256 devices in a mesh: order: 16 (over x, y), lat: 16 (over z, core).
Axes of the slice: x: 4, y: 4, z: 8, core: 2. Of those that a mesh axis runs over, the one named last changes fastest.
Arguments:
- fourier: bfloat16 [512, 64, 2048], P('order', None, 'lat'), may hold values from -6 to 6
- quad_weights: float32 [2048], P('lat'), may hold values from 0.5 to 1.5
- leaf_basis: bfloat16 [512, 64, 2048], P('order', None, 'lat'), may hold values from -0.5 to 0.5
- level_factors: bfloat16 [512, 4, 2, 16, 64, 64], P('order', None, None, 'lat'), may hold values from -0.5 to 0.5
- sparsity: int32 [512, 4, 16], P('order', None, 'lat'), may hold values 0 or 1
- root_basis: bfloat16 [512, 64, 2048], P(None, None, 'lat'), may hold values from -0.75 to 0.75
- order_of_slot: int32 [512], replicated, may hold values from 0 to 511, each once
Outputs:
- spectra: bfloat16 [32, 2, 2048, 512], P('order', None, 'lat')
The draws below stay inside these ranges and needn't reach their ends.
Inputs may be any that keep to these rules, and one draw needn't show every extreme that they name: `order_of_slot`: every window index appears in exactly one slot.
All inputs are finite; a program needn't handle non-finite values. No bound on the sum of `sparsity` on one device may be relied on, other than what follows from the above.
Results may differ from the reference program's by a relative error of at most 0.0081.
Values may be sent and summed in bfloat16 or wider, within the bound.
A program may use at most 64 MiB of HBM per device.

```python
import jax
import jax.numpy as jnp
from jax import lax

DEGREES = 2048
LATS = 2048
FIELDS = 32
RANK = 64
ORDERS = 512
LEVELS = 4
STRIDE = 4
COLS = 64
LAT_DEV = 128
DEG_DEV = 128
N_LAT = 16


def with_ends(values, key, smallest, top_value):
    spot = [jax.random.randint(jax.random.fold_in(key, axis), (), 0, length) for axis, length in enumerate(values.shape)]
    widest = values.shape.index(max(values.shape))
    neighbour = spot[:widest] + [(spot[widest] + 1) % values.shape[widest]] + spot[widest + 1:]
    return values.at[tuple(spot)].set(smallest).at[tuple(neighbour)].set(top_value)


def block_scale(own_key, dims, pieces, smallest, largest):
    def one(position, parts):
        steps = jax.random.uniform(jax.random.fold_in(jax.random.fold_in(own_key, 6), position), (parts,), jnp.float32, smallest / len(pieces), largest / len(pieces))
        return jnp.repeat(jnp.exp(steps), dims[position] // parts).reshape((-1,) + (1,) * (len(dims) - position - 1))

    gain = one(*pieces[0])
    for cut in pieces[1:]:
        gain = gain * one(*cut)
    return gain


def centred(own_key, extent, spread, limit, cuts=(), held_as=jnp.bfloat16):
    result = spread * jax.random.normal(own_key, extent, jnp.float32)
    if cuts:
        result = result * block_scale(own_key, extent, cuts, -0.22, 0.18)
    return jnp.clip(result, -limit, limit).astype(held_as)


def setup_inputs(seed: int = 0) -> dict:
    streams_of = jax.random.split(jax.random.key(seed), 8)
    fourier = centred(streams_of[0], (ORDERS, COLS, LATS), 1.0, 6.0, ((0, 16), (2, 16)))
    quad_weights = jnp.clip(0.5 + 1.0 * jax.random.uniform(streams_of[1], (LATS,), jnp.float32) ** block_scale(streams_of[1], (LATS,), ((0, 16),), -0.2, 0.2), 0.5, 1.5)
    leaf_basis = centred(streams_of[2], (ORDERS, RANK, LATS), (LATS // N_LAT) ** -0.5, 0.5, ((0, 16), (2, 16)))
    level_factors = centred(streams_of[3], (ORDERS, LEVELS, 2, N_LAT, RANK, RANK), (2 * RANK) ** -0.5, 0.5, ((0, 16), (3, 16)))
    sparsity = with_ends((jax.random.randint(streams_of[4], (ORDERS, LEVELS, N_LAT), 0, 4) < 3).astype(jnp.int32), jax.random.fold_in(streams_of[4], 1), 0, 1)
    root_basis = centred(streams_of[5], (ORDERS, RANK, DEGREES), RANK ** -0.5, 0.75, ((2, 16),))
    order_of_slot = jax.random.permutation(streams_of[6], ORDERS).astype(jnp.int32)
    return dict(fourier=fourier, quad_weights=quad_weights, leaf_basis=leaf_basis, level_factors=level_factors, sparsity=sparsity, root_basis=root_basis, order_of_slot=order_of_slot)


def reference(fourier, quad_weights, leaf_basis, level_factors, sparsity, root_basis, order_of_slot):
    blocks = jnp.arange(N_LAT, dtype=jnp.int32)

    def one_order(order_items):
        fourier_one, basis_one, factor_one, mask_one, root_one = order_items
        weighted = (fourier_one.astype(jnp.float32) * quad_weights[None, :]).astype(jnp.bfloat16)
        weighted = weighted.reshape(COLS, N_LAT, LAT_DEV).astype(jnp.float32)
        basis_blocks = basis_one.reshape(RANK, N_LAT, LAT_DEV).astype(jnp.float32)
        rank_state = jnp.einsum("rbj,cbj->brc", basis_blocks, weighted).astype(jnp.bfloat16)
        for depth_bit in range(LEVELS):
            partner = jnp.take(rank_state, blocks ^ (1 << depth_bit), axis=0)
            own_term = jnp.einsum("bst,btc->bsc", factor_one[depth_bit, 0].astype(jnp.float32), rank_state.astype(jnp.float32))
            cross_term = jnp.einsum("bst,btc->bsc", factor_one[depth_bit, 1].astype(jnp.float32), partner.astype(jnp.float32))
            present = mask_one[depth_bit].astype(jnp.float32)[:, None, None]
            rank_state = (own_term + present * cross_term).astype(jnp.bfloat16)
        root_blocks = root_one.reshape(RANK, N_LAT, DEG_DEV).astype(jnp.float32)
        coefficient = jnp.einsum("rbl,brc->blc", root_blocks, rank_state.astype(jnp.float32)).astype(jnp.bfloat16)
        return coefficient.reshape(DEGREES, COLS)

    coeffs = lax.map(one_order, (fourier, leaf_basis, level_factors, sparsity, root_basis))
    natural = jnp.zeros_like(coeffs).at[order_of_slot].set(coeffs)
    degree = jnp.arange(DEGREES, dtype=jnp.int32)
    window = STRIDE * jnp.arange(ORDERS, dtype=jnp.int32)
    alive_mask = degree[None, :, None] >= window[:, None, None]
    masked = jnp.where(alive_mask, natural, jnp.zeros((), natural.dtype))
    return masked.reshape(ORDERS, DEGREES, FIELDS, 2).transpose(2, 3, 1, 0)
```

```python
import functools

import jax
import jax.numpy as jnp
from jax import lax
from jax.experimental import pallas as pl
from jax.experimental.pallas import tpu as pltpu
from jax.sharding import PartitionSpec as P

DEGREES = 2048
MESH = pl.DeviceIdType.MESH
BF16 = jnp.bfloat16
F32 = jnp.float32
I32 = jnp.int32

SLOTS = 32
CHUNK = 4
CHUNKS = SLOTS // CHUNK
LEVELS = 4
GROUPS = 4
N_ORDER = 16
RANK = 64


def schedule():
    events = []
    keyed = []
    for c in range(CHUNKS):
        keyed.append((c * 1.0, 0, ("s", 0, c)))
        keyed.append((c * 1.0 + 2.5, 1, ("s", 1, c)))
        keyed.append((c * 1.0 + 5.5, 2, ("s", 2, c)))
        keyed.append((c * 2.0 + 12.0, 3, ("s", 3, c)))
        keyed.append((c * 2.0 + 18.5, 4, ("s", 4, c)))
    for g in range(GROUPS):
        keyed.append(((2 * g + 1) * 2.0 + 18.6, 5, ("a", g)))
        keyed.append(((2 * g + 1) * 2.0 + 18.6 + 3.5, 6, ("r", g)))
    keyed.append((8.1, 7, ("p",)))
    for _, _, event in sorted(keyed):
        events.append(event)
    return events


def kernel(
    four_hbm, quad_hbm, leaf_hbm, fac_hbm, spars_hbm, root_hbm, order_hbm, out_hbm,
    four, quad, leaf, fac, spars, root, order, out,
    state, partner, own, perm, send_buf, recv_buf, order_col, pick, coef, coef_t,
    in_sem, small_sem, root_sem, out_sem, send_sem, recv_sem, a2a_send_sem, a2a_recv_sem,
):
    me_o = lax.axis_index("order")
    me_l = lax.axis_index("lat")
    peers = [me_l ^ (1 << k) for k in range(LEVELS)]

    def loads(c):
        span = pl.ds(c * CHUNK, CHUNK)
        return [
            pltpu.make_async_copy(four_hbm.at[span], four.at[span], in_sem.at[0, c]),
            pltpu.make_async_copy(leaf_hbm.at[span], leaf.at[span], in_sem.at[1, c]),
            pltpu.make_async_copy(fac_hbm.at[span, :, :, 0], fac.at[span], in_sem.at[2, c]),
        ]

    small = [
        pltpu.make_async_copy(quad_hbm, quad, small_sem.at[0]),
        pltpu.make_async_copy(spars_hbm, spars, small_sem.at[1]),
        pltpu.make_async_copy(order_hbm, order, small_sem.at[2]),
    ]
    root_copy = pltpu.make_async_copy(root_hbm, root, root_sem)
    all_loads = [loads(c) for c in range(CHUNKS)]
    for copy in small:
        copy.start()
    for c in range(CHUNKS):
        for copy in all_loads[c]:
            copy.start()
    root_copy.start()

    barrier = pltpu.get_barrier_semaphore()
    for peer in peers:
        pl.semaphore_signal(barrier, inc=1, device_id=(me_o, peer), device_id_type=MESH)
    for i in range(1, N_ORDER):
        pl.semaphore_signal(
            barrier, inc=1, device_id=(lax.rem(me_o + i, N_ORDER), me_l), device_id_type=MESH
        )

    def level_copy(k, c):
        return pltpu.make_async_remote_copy(
            src_ref=state.at[k, c],
            dst_ref=partner.at[k, c],
            send_sem=send_sem.at[k, c],
            recv_sem=recv_sem.at[k, c],
            device_id=(me_o, peers[k]),
            device_id_type=MESH,
        )

    def a2a_copy(g, dest, source):
        return pltpu.make_async_remote_copy(
            src_ref=send_buf.at[g, dest],
            dst_ref=recv_buf.at[g, source],
            send_sem=a2a_send_sem.at[g, dest],
            recv_sem=a2a_recv_sem.at[g, source],
            device_id=(dest, me_l),
            device_id_type=MESH,
        )

    low = lax.broadcasted_iota(I32, (RANK, 128), 1) < RANK

    def both(a, b):
        return jnp.concatenate([a, b], axis=0)

    def diagonal(product):
        return jnp.where(low, product[:RANK], product[RANK:])

    def own_terms(k, c):
        for h in range(2):
            s0, s1 = c * CHUNK + h, c * CHUNK + 2 + h
            a = both(fac[s0, k, 0], fac[s1, k, 0])
            own[k, c, h] = diagonal(jnp.dot(a, state[k, c, h], preferred_element_type=F32))

    def start_event(c):
        for copy in all_loads[c][:2]:
            copy.wait()
        w = quad[...]
        for h in range(2):
            s0, s1 = c * CHUNK + h, c * CHUNK + 2 + h
            weighted = both(
                (four[s0].astype(F32) * w).astype(BF16), (four[s1].astype(F32) * w).astype(BF16)
            )
            basis = both(leaf[s0], leaf[s1])
            product = lax.dot_general(
                basis, weighted, (((1,), (1,)), ((), ())), preferred_element_type=F32
            )
            state[0, c, h] = diagonal(product).astype(BF16)

    def level_event(k, c):
        level_copy(k, c).wait_recv()
        for h in range(2):
            s0, s1 = c * CHUNK + h, c * CHUNK + 2 + h
            b = both(fac[s0, k, 1], fac[s1, k, 1])
            cross = diagonal(jnp.dot(b, partner[k, c, h], preferred_element_type=F32))
            present = jnp.where(low, spars[k, 0, s0], spars[k, 0, s1]).astype(F32)
            state[k + 1, c, h] = (own[k, c, h] + present * cross).astype(BF16)

    def a2a_event(g):
        x = jnp.concatenate(
            [
                state[LEVELS, 2 * g].reshape(2 * RANK, 128),
                state[LEVELS, 2 * g + 1].reshape(2 * RANK, 128),
            ],
            axis=1,
        )
        packed = lax.dot_general(
            perm[...], x, (((1,), (1,)), ((), ())), preferred_element_type=F32
        ).astype(BF16)
        send_buf[g] = packed.reshape(N_ORDER, 16, 128)

        def one(i, carry):
            a2a_copy(g, lax.rem(me_o + i, N_ORDER), me_o).start()
            return carry

        lax.fori_loop(1, N_ORDER, one, 0)
        recv_buf[g, me_o] = send_buf[g, me_o]

    def prepare_perm():
        row = lax.broadcasted_iota(I32, (256, 256), 0)
        col = lax.broadcasted_iota(I32, (256, 256), 1)
        target = (row & 3) * 64 + (row >> 4) * 4 + ((row >> 2) & 3)
        perm[...] = (col == target).astype(F32).astype(BF16)

    def prepare_pick():
        small[2].wait()
        orders = order[...].astype(F32)
        for i in range(4):
            wide = jnp.broadcast_to(orders[i : i + 1], (128, 128))
            order_col[pl.ds(i * 128, 128)] = wide.T
        window = lax.broadcasted_iota(I32, (16, 512), 1).astype(F32)
        for g in range(GROUPS):
            for q in range(4):
                for h in range(2):
                    col = order_col[pl.ds(8 * g + 2 * q + h, 16, stride=SLOTS), :]
                    wide = jnp.concatenate([col] * 4, axis=1)
                    row = g * 128 + q * 32 + h * 16
                    pick[pl.ds(row, 16)] = (wide == window).astype(F32).astype(BF16)

    def root_event(g):
        if g == 0:
            root_copy.wait()

        def arrived(i, carry):
            source = lax.rem(me_o + i, N_ORDER)
            a2a_copy(g, source, source).wait_recv()
            return carry

        lax.fori_loop(1, N_ORDER, arrived, 0)

        row = lax.broadcasted_iota(I32, (32, 256), 0)
        col = lax.broadcasted_iota(I32, (32, 256), 1)
        keep = ((row >> 4) == ((col >> 6) & 1)) & ((row & 1) == (col >> 7))
        keep = keep.astype(F32).astype(BF16)
        first = (lax.broadcasted_iota(I32, (32, 128), 0) & 2) == 0

        def one(source, carry):
            r = recv_buf[g, source]
            r2 = jnp.concatenate([r, r], axis=1)
            lhs = jnp.concatenate([r2, r2], axis=0) * keep
            base = source * SLOTS + 8 * g
            wa = root[pl.ds(base, 4)].reshape(256, 128)
            wb = root[pl.ds(base + 4, 4)].reshape(256, 128)
            product = jnp.dot(
                lhs, jnp.concatenate([wa, wb], axis=1), preferred_element_type=F32
            )
            coef[pl.ds(pl.multiple_of(source * 32, 32), 32)] = jnp.where(
                first, product[:, :128], product[:, 128:]
            )
            return carry

        lax.fori_loop(0, N_ORDER, one, 0, unroll=4)
        for cc in range(4):
            parts = []
            for q in range(4):
                for h in range(2):
                    parts.append(coef[pl.ds(h * 16 + cc * 4 + q, 16, stride=32), :])
            coef_t[cc, :, pl.ds(g * 128, 128)] = jnp.concatenate(parts, axis=0).T.astype(BF16)

    def finish():
        degree = me_l * 128 + lax.broadcasted_iota(I32, (128, 512), 0)
        window = DEGREES // 512 * lax.broadcasted_iota(I32, (128, 512), 1)
        alive = degree >= window
        copies = []
        for cc in range(4):
            natural = jnp.dot(coef_t[cc], pick[...], preferred_element_type=F32)
            out[cc // 2, cc % 2] = jnp.where(alive, natural, 0.0).astype(BF16)
            copy = pltpu.make_async_copy(
                out.at[cc // 2, cc % 2], out_hbm.at[cc // 2, cc % 2], out_sem.at[cc]
            )
            copy.start()
            copies.append(copy)
        return copies

    small[0].wait()
    passed = False
    for event in schedule():
        if event[0] == "s" and event[1] == 0:
            c = event[2]
            start_event(c)
            if not passed:
                pl.semaphore_wait(barrier, LEVELS + N_ORDER - 1)
                small[1].wait()
                passed = True
            level_copy(0, c).start()
            all_loads[c][2].wait()
            own_terms(0, c)
        elif event[0] == "s":
            _, k, c = event
            level_event(k - 1, c)
            if k < LEVELS:
                level_copy(k, c).start()
                own_terms(k, c)
        elif event[0] == "a":
            a2a_event(event[1])
        elif event[0] == "p":
            prepare_perm()
            prepare_pick()
        else:
            root_event(event[1])
    out_copies = finish()
    for k in range(LEVELS):
        for c in range(CHUNKS):
            level_copy(k, c).wait_send()
    for g in range(GROUPS):

        def sent(i, carry):
            a2a_copy(g, lax.rem(me_o + i, N_ORDER), me_o).wait_send()
            return carry

        lax.fori_loop(1, N_ORDER, sent, 0)
    for copy in out_copies:
        copy.wait()


def per_device(
    fourier, quad_weights, leaf_basis, level_factors, sparsity, root_basis, order_of_slot
):
    anywhere = pl.BlockSpec(memory_space=pl.ANY)
    vmem = pltpu.VMEM
    return pl.pallas_call(
        kernel,
        out_shape=jax.ShapeDtypeStruct((2, 2, 128, 512), BF16),
        in_specs=[anywhere] * 7,
        out_specs=anywhere,
        scratch_shapes=[
            vmem((SLOTS, 64, 128), BF16),
            vmem((1, 128), F32),
            vmem((SLOTS, 64, 128), BF16),
            vmem((SLOTS, LEVELS, 2, 64, 64), BF16),
            pltpu.SMEM((LEVELS, 1, SLOTS), I32),
            vmem((512, 64, 128), BF16),
            vmem((4, 128), I32),
            vmem((2, 2, 128, 512), BF16),
            vmem((LEVELS + 1, CHUNKS, 2, RANK, 128), BF16),
            vmem((LEVELS, CHUNKS, 2, RANK, 128), BF16),
            vmem((LEVELS, CHUNKS, 2, RANK, 128), F32),
            vmem((256, 256), BF16),
            vmem((GROUPS, N_ORDER, 16, 128), BF16),
            vmem((GROUPS, N_ORDER, 16, 128), BF16),
            vmem((512, 128), F32),
            vmem((512, 512), BF16),
            vmem((512, 128), F32),
            vmem((4, 128, 512), BF16),
            pltpu.SemaphoreType.DMA((3, CHUNKS)),
            pltpu.SemaphoreType.DMA((3,)),
            pltpu.SemaphoreType.DMA,
            pltpu.SemaphoreType.DMA((4,)),
            pltpu.SemaphoreType.DMA((LEVELS, CHUNKS)),
            pltpu.SemaphoreType.DMA((LEVELS, CHUNKS)),
            pltpu.SemaphoreType.DMA((GROUPS, N_ORDER)),
            pltpu.SemaphoreType.DMA((GROUPS, N_ORDER)),
        ],
        compiler_params=pltpu.CompilerParams(
            collective_id=0, has_side_effects=True, vmem_limit_bytes=48 * 1024 * 1024
        ),
        cost_estimate=pl.CostEstimate(
            flops=2 * 10**9, bytes_accessed=15 * 10**6, transcendentals=0
        ),
    )(
        fourier,
        quad_weights.reshape(1, 128),
        leaf_basis,
        level_factors,
        sparsity.transpose(1, 2, 0),
        root_basis,
        order_of_slot.reshape(4, 128),
    )


def solution(mesh):
    return jax.shard_map(
        per_device,
        mesh=mesh,
        in_specs=(
            P("order", None, "lat"),
            P("lat"),
            P("order", None, "lat"),
            P("order", None, None, "lat", None, None),
            P("order", None, "lat"),
            P(None, None, "lat"),
            P(),
        ),
        out_specs=P("order", None, "lat", None),
        check_vma=False,
    )
```

```python
import functools

import jax
import jax.numpy as jnp
from jax import lax
from jax.experimental import pallas as pl
from jax.experimental.pallas import tpu as pltpu
from jax.sharding import PartitionSpec as P

DEGREES = 2048
MESH = pl.DeviceIdType.MESH
BF16 = jnp.bfloat16
F32 = jnp.float32
I32 = jnp.int32

SLOTS = 32
CHUNK = 4
CHUNKS = SLOTS // CHUNK
LEVELS = 4
GROUPS = 4
N_ORDER = 16
RANK = 64


def schedule():
    events = []
    keyed = []
    for c in range(CHUNKS):
        keyed.append((c * 1.0, 0, ("s", 0, c)))
        keyed.append((c * 1.0 + 2.5, 1, ("s", 1, c)))
        keyed.append((c * 1.0 + 5.5, 2, ("s", 2, c)))
        keyed.append((c * 2.0 + 12.0, 3, ("s", 3, c)))
        keyed.append((c * 2.0 + 18.5, 4, ("s", 4, c)))
    for g in range(GROUPS):
        keyed.append(((2 * g + 1) * 2.0 + 18.6, 5, ("a", g)))
        keyed.append(((2 * g + 1) * 2.0 + 18.6 + 3.5, 6, ("r", g)))
    keyed.append((8.1, 7, ("p",)))
    for _, _, event in sorted(keyed):
        events.append(event)
    return events


def kernel(
    four_hbm, quad_hbm, leaf_hbm, fac_hbm, spars_hbm, root_hbm, order_hbm, out_hbm,
    four, quad, leaf, fac, spars, root, order, out,
    state, partner, own, perm, send_buf, recv_buf, order_col, pick, coef, coef_t,
    in_sem, small_sem, root_sem, out_sem, send_sem, recv_sem, a2a_send_sem, a2a_recv_sem,
):
    me_o = lax.axis_index("order")
    me_l = lax.axis_index("lat")
    peers = [me_l ^ (1 << k) for k in range(LEVELS)]

    def loads(c):
        span = pl.ds(c * CHUNK, CHUNK)
        return [
            pltpu.make_async_copy(four_hbm.at[span], four.at[span], in_sem.at[0, c]),
            pltpu.make_async_copy(leaf_hbm.at[span], leaf.at[span], in_sem.at[1, c]),
            pltpu.make_async_copy(fac_hbm.at[span, :, :, 0], fac.at[span], in_sem.at[2, c]),
        ]

    small = [
        pltpu.make_async_copy(quad_hbm, quad, small_sem.at[0]),
        pltpu.make_async_copy(spars_hbm, spars, small_sem.at[1]),
        pltpu.make_async_copy(order_hbm, order, small_sem.at[2]),
    ]
    root_copy = pltpu.make_async_copy(root_hbm, root, root_sem)
    all_loads = [loads(c) for c in range(CHUNKS)]
    for copy in small:
        copy.start()
    for c in range(CHUNKS):
        for copy in all_loads[c]:
            copy.start()
    root_copy.start()

    barrier = pltpu.get_barrier_semaphore()
    for peer in peers:
        pl.semaphore_signal(barrier, inc=1, device_id=(me_o, peer), device_id_type=MESH)
    for i in range(1, N_ORDER):
        pl.semaphore_signal(
            barrier, inc=1, device_id=(lax.rem(me_o + i, N_ORDER), me_l), device_id_type=MESH
        )

    def level_copy(k, c):
        return pltpu.make_async_remote_copy(
            src_ref=state.at[k, c],
            dst_ref=partner.at[k, c],
            send_sem=send_sem.at[k, c],
            recv_sem=recv_sem.at[k, c],
            device_id=(me_o, peers[k]),
            device_id_type=MESH,
        )

    shifted = [lax.rem(me_o + i, N_ORDER) for i in range(N_ORDER)]
    others = pl.ds(1, N_ORDER - 1)

    def a2a_copy(g, i):
        return pltpu.make_async_remote_copy(
            src_ref=send_buf.at[g, shifted[i]],
            dst_ref=recv_buf.at[g, i],
            send_sem=a2a_send_sem.at[g],
            recv_sem=a2a_recv_sem.at[g],
            device_id=(shifted[i], me_l),
            device_id_type=MESH,
        )

    def a2a_all(g):
        return pltpu.make_async_remote_copy(
            src_ref=send_buf.at[g, others],
            dst_ref=recv_buf.at[g, others],
            send_sem=a2a_send_sem.at[g],
            recv_sem=a2a_recv_sem.at[g],
            device_id=(shifted[1], me_l),
            device_id_type=MESH,
        )

    low = lax.broadcasted_iota(I32, (RANK, 128), 1) < RANK

    def both(a, b):
        return jnp.concatenate([a, b], axis=0)

    def diagonal(product):
        return jnp.where(low, product[:RANK], product[RANK:])

    def own_terms(k, c):
        for h in range(2):
            s0, s1 = c * CHUNK + h, c * CHUNK + 2 + h
            a = both(fac[s0, k, 0], fac[s1, k, 0])
            own[k, c, h] = diagonal(jnp.dot(a, state[k, c, h], preferred_element_type=F32))

    def start_event(c):
        for copy in all_loads[c][:2]:
            copy.wait()
        w = quad[...]
        for h in range(2):
            s0, s1 = c * CHUNK + h, c * CHUNK + 2 + h
            weighted = both(
                (four[s0].astype(F32) * w).astype(BF16), (four[s1].astype(F32) * w).astype(BF16)
            )
            basis = both(leaf[s0], leaf[s1])
            product = lax.dot_general(
                basis, weighted, (((1,), (1,)), ((), ())), preferred_element_type=F32
            )
            state[0, c, h] = diagonal(product).astype(BF16)

    def level_event(k, c):
        level_copy(k, c).wait_recv()
        for h in range(2):
            s0, s1 = c * CHUNK + h, c * CHUNK + 2 + h
            b = both(fac[s0, k, 1], fac[s1, k, 1])
            cross = diagonal(jnp.dot(b, partner[k, c, h], preferred_element_type=F32))
            present = jnp.where(low, spars[k, 0, s0], spars[k, 0, s1]).astype(F32)
            state[k + 1, c, h] = (own[k, c, h] + present * cross).astype(BF16)

    def a2a_event(g):
        x = jnp.concatenate(
            [
                state[LEVELS, 2 * g].reshape(2 * RANK, 128),
                state[LEVELS, 2 * g + 1].reshape(2 * RANK, 128),
            ],
            axis=1,
        )
        packed = lax.dot_general(
            perm[...], x, (((1,), (1,)), ((), ())), preferred_element_type=F32
        ).astype(BF16)
        send_buf[g] = packed.reshape(N_ORDER, 16, 128)

        for i in range(1, N_ORDER):
            a2a_copy(g, i).start()
        recv_buf[g, 0] = send_buf[g, me_o]

    def prepare_perm():
        row = lax.broadcasted_iota(I32, (256, 256), 0)
        col = lax.broadcasted_iota(I32, (256, 256), 1)
        target = (row & 3) * 64 + (row >> 4) * 4 + ((row >> 2) & 3)
        perm[...] = (col == target).astype(F32).astype(BF16)

    def prepare_pick():
        small[2].wait()
        orders = order[...].astype(F32)
        for i in range(4):
            wide = jnp.broadcast_to(orders[i : i + 1], (128, 128))
            order_col[pl.ds(i * 128, 128)] = wide.T
        window = lax.broadcasted_iota(I32, (16, 512), 1).astype(F32)
        for g in range(GROUPS):
            for q in range(4):
                for h in range(2):
                    col = order_col[pl.ds(8 * g + 2 * q + h, 16, stride=SLOTS), :]
                    wide = jnp.concatenate([col] * 4, axis=1)
                    row = g * 128 + q * 32 + h * 16
                    pick[pl.ds(row, 16)] = (wide == window).astype(F32).astype(BF16)

    def root_event(g):
        if g == 0:
            root_copy.wait()

        a2a_all(g).wait_recv()

        row = lax.broadcasted_iota(I32, (32, 256), 0)
        col = lax.broadcasted_iota(I32, (32, 256), 1)
        keep = ((row >> 4) == ((col >> 6) & 1)) & ((row & 1) == (col >> 7))
        keep = keep.astype(F32).astype(BF16)
        first = (lax.broadcasted_iota(I32, (32, 128), 0) & 2) == 0

        def one(i, carry):
            source = lax.rem(me_o - i + N_ORDER, N_ORDER)
            r = recv_buf[g, i]
            r2 = jnp.concatenate([r, r], axis=1)
            lhs = jnp.concatenate([r2, r2], axis=0) * keep
            base = source * SLOTS + 8 * g
            wa = root[pl.ds(base, 4)].reshape(256, 128)
            wb = root[pl.ds(base + 4, 4)].reshape(256, 128)
            product = jnp.dot(
                lhs, jnp.concatenate([wa, wb], axis=1), preferred_element_type=F32
            )
            coef[pl.ds(pl.multiple_of(source * 32, 32), 32)] = jnp.where(
                first, product[:, :128], product[:, 128:]
            )
            return carry

        lax.fori_loop(0, N_ORDER, one, 0, unroll=4)
        for cc in range(4):
            parts = []
            for q in range(4):
                for h in range(2):
                    parts.append(coef[pl.ds(h * 16 + cc * 4 + q, 16, stride=32), :])
            coef_t[cc, :, pl.ds(g * 128, 128)] = jnp.concatenate(parts, axis=0).T.astype(BF16)

    def finish():
        degree = me_l * 128 + lax.broadcasted_iota(I32, (128, 512), 0)
        window = DEGREES // 512 * lax.broadcasted_iota(I32, (128, 512), 1)
        alive = degree >= window
        copies = []
        for cc in range(4):
            natural = jnp.dot(coef_t[cc], pick[...], preferred_element_type=F32)
            out[cc // 2, cc % 2] = jnp.where(alive, natural, 0.0).astype(BF16)
            copy = pltpu.make_async_copy(
                out.at[cc // 2, cc % 2], out_hbm.at[cc // 2, cc % 2], out_sem.at[cc]
            )
            copy.start()
            copies.append(copy)
        return copies

    small[0].wait()
    passed = False
    for event in schedule():
        if event[0] == "s" and event[1] == 0:
            c = event[2]
            start_event(c)
            if not passed:
                pl.semaphore_wait(barrier, LEVELS + N_ORDER - 1)
                small[1].wait()
                passed = True
            level_copy(0, c).start()
            all_loads[c][2].wait()
            own_terms(0, c)
        elif event[0] == "s":
            _, k, c = event
            level_event(k - 1, c)
            if k < LEVELS:
                level_copy(k, c).start()
                own_terms(k, c)
        elif event[0] == "a":
            a2a_event(event[1])
        elif event[0] == "p":
            prepare_perm()
            prepare_pick()
        else:
            root_event(event[1])
    out_copies = finish()
    for k in range(LEVELS):
        for c in range(CHUNKS):
            level_copy(k, c).wait_send()
    for g in range(GROUPS):
        a2a_all(g).wait_send()
    for copy in out_copies:
        copy.wait()


def per_device(
    fourier, quad_weights, leaf_basis, level_factors, sparsity, root_basis, order_of_slot
):
    anywhere = pl.BlockSpec(memory_space=pl.ANY)
    vmem = pltpu.VMEM
    return pl.pallas_call(
        kernel,
        out_shape=jax.ShapeDtypeStruct((2, 2, 128, 512), BF16),
        in_specs=[anywhere] * 7,
        out_specs=anywhere,
        scratch_shapes=[
            vmem((SLOTS, 64, 128), BF16),
            vmem((1, 128), F32),
            vmem((SLOTS, 64, 128), BF16),
            vmem((SLOTS, LEVELS, 2, 64, 64), BF16),
            pltpu.SMEM((LEVELS, 1, SLOTS), I32),
            vmem((512, 64, 128), BF16),
            vmem((4, 128), I32),
            vmem((2, 2, 128, 512), BF16),
            vmem((LEVELS + 1, CHUNKS, 2, RANK, 128), BF16),
            vmem((LEVELS, CHUNKS, 2, RANK, 128), BF16),
            vmem((LEVELS, CHUNKS, 2, RANK, 128), F32),
            vmem((256, 256), BF16),
            vmem((GROUPS, N_ORDER, 16, 128), BF16),
            vmem((GROUPS, N_ORDER, 16, 128), BF16),
            vmem((512, 128), F32),
            vmem((512, 512), BF16),
            vmem((512, 128), F32),
            vmem((4, 128, 512), BF16),
            pltpu.SemaphoreType.DMA((3, CHUNKS)),
            pltpu.SemaphoreType.DMA((3,)),
            pltpu.SemaphoreType.DMA,
            pltpu.SemaphoreType.DMA((4,)),
            pltpu.SemaphoreType.DMA((LEVELS, CHUNKS)),
            pltpu.SemaphoreType.DMA((LEVELS, CHUNKS)),
            pltpu.SemaphoreType.DMA((GROUPS,)),
            pltpu.SemaphoreType.DMA((GROUPS,)),
        ],
        compiler_params=pltpu.CompilerParams(
            collective_id=0, has_side_effects=True, vmem_limit_bytes=60 * 1024 * 1024
        ),
        cost_estimate=pl.CostEstimate(
            flops=2 * 10**9, bytes_accessed=15 * 10**6, transcendentals=0
        ),
    )(
        fourier,
        quad_weights.reshape(1, 128),
        leaf_basis,
        level_factors,
        sparsity.transpose(1, 2, 0),
        root_basis,
        order_of_slot.reshape(4, 128),
    )


def solution(mesh):
    return jax.shard_map(
        per_device,
        mesh=mesh,
        in_specs=(
            P("order", None, "lat"),
            P("lat"),
            P("order", None, "lat"),
            P("order", None, None, "lat", None, None),
            P("order", None, "lat"),
            P(None, None, "lat"),
            P(),
        ),
        out_specs=P("order", None, "lat", None),
        check_vma=False,
    )
```

```python
import functools

import jax
import jax.numpy as jnp
from jax import lax
from jax.experimental import pallas as pl
from jax.experimental.pallas import tpu as pltpu
from jax.sharding import PartitionSpec as P

DEGREES = 2048
MESH = pl.DeviceIdType.MESH
BF16 = jnp.bfloat16
F32 = jnp.float32
I32 = jnp.int32

SLOTS = 32
CHUNK = 4
CHUNKS = SLOTS // CHUNK
LEVELS = 4
GROUPS = 4
N_ORDER = 16
RANK = 64


def schedule():

    keyed = []
    for c in range(CHUNKS):
        keyed.append((c * 1.0, 0, ("s", 0, c)))
        keyed.append((c * 1.0 + 2.5, 1, ("s", 1, c)))
        keyed.append((c * 1.0 + 5.5, 2, ("s", 2, c)))
        keyed.append((c * 2.0 + 12.0, 3, ("s", 3, c)))
        keyed.append((c * 2.0 + 18.5, 4, ("s", 4, c)))
    for g in range(GROUPS):
        keyed.append(((2 * g + 1) * 2.0 + 18.5 + 0.1, 5, ("a", g)))
        keyed.append((99 + g, 6, ("r", g)))
    keyed.append((8.1, 7, ("p",)))
    return [e for _, _, e in sorted(keyed)]


def kernel(
    four_hbm, quad_hbm, leaf_hbm, fac_hbm, spars_hbm, root_hbm, order_hbm, out_hbm,
    four, quad, leaf, fac, spars, root, order, out,
    state, partner, own, perm, send_buf, recv_buf, order_col, pick, coef, coef_t,
    in_sem, small_sem, root_sem, out_sem, send_sem, recv_sem, a2a_send_sem, a2a_recv_sem,
):
    me_o = lax.axis_index("order")
    me_l = lax.axis_index("lat")
    peers = [me_l ^ (1 << k) for k in range(LEVELS)]

    def loads(c):
        span = pl.ds(c * CHUNK, CHUNK)
        return [
            pltpu.make_async_copy(four_hbm.at[span], four.at[span], in_sem.at[0, c]),
            pltpu.make_async_copy(leaf_hbm.at[span], leaf.at[span], in_sem.at[1, c]),
            pltpu.make_async_copy(fac_hbm.at[span, :, :, 0], fac.at[span], in_sem.at[2, c]),
        ]

    small = [
        pltpu.make_async_copy(quad_hbm, quad, small_sem.at[0]),
        pltpu.make_async_copy(spars_hbm, spars, small_sem.at[1]),
        pltpu.make_async_copy(order_hbm, order, small_sem.at[2]),
    ]
    root_copy = pltpu.make_async_copy(root_hbm, root, root_sem)
    all_loads = [loads(c) for c in range(CHUNKS)]
    for copy in small:
        copy.start()
    for c in range(CHUNKS):
        for copy in all_loads[c]:
            copy.start()
    root_copy.start()

    barrier = pltpu.get_barrier_semaphore()
    for peer in peers:
        pl.semaphore_signal(barrier, inc=1, device_id=(me_o, peer), device_id_type=MESH)
    for i in range(1, N_ORDER):
        pl.semaphore_signal(
            barrier, inc=1, device_id=(lax.rem(me_o + i, N_ORDER), me_l), device_id_type=MESH
        )

    def level_copy(k, c):
        return pltpu.make_async_remote_copy(
            src_ref=state.at[k, c],
            dst_ref=partner.at[k, c],
            send_sem=send_sem.at[k, c],
            recv_sem=recv_sem.at[k, c],
            device_id=(me_o, peers[k]),
            device_id_type=MESH,
        )

    shifted = [lax.rem(me_o + i, N_ORDER) for i in range(N_ORDER)]
    others = pl.ds(1, N_ORDER - 1)

    def a2a_copy(g, i):
        return pltpu.make_async_remote_copy(
            src_ref=send_buf.at[g, shifted[i]],
            dst_ref=recv_buf.at[g, i],
            send_sem=a2a_send_sem.at[g],
            recv_sem=a2a_recv_sem.at[g],
            device_id=(shifted[i], me_l),
            device_id_type=MESH,
        )

    def a2a_all(g):
        return pltpu.make_async_remote_copy(
            src_ref=send_buf.at[g, others],
            dst_ref=recv_buf.at[g, others],
            send_sem=a2a_send_sem.at[g],
            recv_sem=a2a_recv_sem.at[g],
            device_id=(shifted[1], me_l),
            device_id_type=MESH,
        )

    low = lax.broadcasted_iota(I32, (RANK, 128), 1) < RANK

    def both(a, b):
        return jnp.concatenate([a, b], axis=0)

    def diagonal(product):
        return jnp.where(low, product[:RANK], product[RANK:])

    def own_terms(k, c):
        for h in range(2):
            s0, s1 = c * CHUNK + h, c * CHUNK + 2 + h
            a = both(fac[s0, k, 0], fac[s1, k, 0])
            own[k, c, h] = diagonal(jnp.dot(a, state[k, c, h], preferred_element_type=F32))

    def start_event(c):
        for copy in all_loads[c][:2]:
            copy.wait()
        w = quad[...]
        for h in range(2):
            s0, s1 = c * CHUNK + h, c * CHUNK + 2 + h
            weighted = both(
                (four[s0].astype(F32) * w).astype(BF16), (four[s1].astype(F32) * w).astype(BF16)
            )
            basis = both(leaf[s0], leaf[s1])
            product = lax.dot_general(
                basis, weighted, (((1,), (1,)), ((), ())), preferred_element_type=F32
            )
            state[0, c, h] = diagonal(product).astype(BF16)

    def level_event(k, c):
        level_copy(k, c).wait_recv()
        for h in range(2):
            s0, s1 = c * CHUNK + h, c * CHUNK + 2 + h
            b = both(fac[s0, k, 1], fac[s1, k, 1])
            cross = diagonal(jnp.dot(b, partner[k, c, h], preferred_element_type=F32))
            present = jnp.where(low, spars[k, 0, s0], spars[k, 0, s1]).astype(F32)
            state[k + 1, c, h] = (own[k, c, h] + present * cross).astype(BF16)

    def a2a_event(g):
        x = jnp.concatenate(
            [
                state[LEVELS, 2 * g].reshape(2 * RANK, 128),
                state[LEVELS, 2 * g + 1].reshape(2 * RANK, 128),
            ],
            axis=1,
        )
        packed = lax.dot_general(
            perm[...], x, (((1,), (1,)), ((), ())), preferred_element_type=F32
        ).astype(BF16)
        send_buf[g] = packed.reshape(N_ORDER, 16, 128)

        for i in range(1, N_ORDER):
            a2a_copy(g, i).start()
        recv_buf[g, 0] = send_buf[g, me_o]

    def prepare_perm():
        row = lax.broadcasted_iota(I32, (256, 256), 0)
        col = lax.broadcasted_iota(I32, (256, 256), 1)
        target = (row & 3) * 64 + (row >> 4) * 4 + ((row >> 2) & 3)
        perm[...] = (col == target).astype(F32).astype(BF16)

    def prepare_pick():
        small[2].wait()
        orders = order[...].astype(F32)
        for i in range(4):
            wide = jnp.broadcast_to(orders[i : i + 1], (128, 128))
            order_col[pl.ds(i * 128, 128)] = wide.T
        window = lax.broadcasted_iota(I32, (16, 512), 1).astype(F32)
        for g in range(GROUPS):
            for q in range(4):
                for h in range(2):
                    col = order_col[pl.ds(8 * g + 2 * q + h, 16, stride=SLOTS), :]
                    wide = jnp.concatenate([col] * 4, axis=1)
                    row = g * 128 + q * 32 + h * 16
                    pick[pl.ds(row, 16)] = (wide == window).astype(F32).astype(BF16)

    def root_event(g):
        if g == 0:
            root_copy.wait()

        a2a_all(g).wait_recv()

        row = lax.broadcasted_iota(I32, (32, 256), 0)
        col = lax.broadcasted_iota(I32, (32, 256), 1)
        keep = ((row >> 4) == ((col >> 6) & 1)) & ((row & 1) == (col >> 7))
        keep = keep.astype(F32).astype(BF16)
        first = (lax.broadcasted_iota(I32, (32, 128), 0) & 2) == 0

        def one(i, carry):
            source = lax.rem(me_o - i + N_ORDER, N_ORDER)
            r = recv_buf[g, i]
            r2 = jnp.concatenate([r, r], axis=1)
            lhs = jnp.concatenate([r2, r2], axis=0) * keep
            base = source * SLOTS + 8 * g
            wa = root[pl.ds(base, 4)].reshape(256, 128)
            wb = root[pl.ds(base + 4, 4)].reshape(256, 128)
            product = jnp.dot(
                lhs, jnp.concatenate([wa, wb], axis=1), preferred_element_type=F32
            )
            coef[pl.ds(pl.multiple_of(source * 32, 32), 32)] = jnp.where(
                first, product[:, :128], product[:, 128:]
            )
            return carry

        lax.fori_loop(0, N_ORDER, one, 0, unroll=4)
        for cc in range(4):
            parts = []
            for q in range(4):
                for h in range(2):
                    parts.append(coef[pl.ds(h * 16 + cc * 4 + q, 16, stride=32), :])
            coef_t[cc, :, pl.ds(g * 128, 128)] = jnp.concatenate(parts, axis=0).T.astype(BF16)

    def finish():
        degree = me_l * 128 + lax.broadcasted_iota(I32, (128, 512), 0)
        window = DEGREES // 512 * lax.broadcasted_iota(I32, (128, 512), 1)
        alive = degree >= window
        copies = []
        for cc in range(4):
            natural = jnp.dot(coef_t[cc], pick[...], preferred_element_type=F32)
            out[cc // 2, cc % 2] = jnp.where(alive, natural, 0.0).astype(BF16)
            copy = pltpu.make_async_copy(
                out.at[cc // 2, cc % 2], out_hbm.at[cc // 2, cc % 2], out_sem.at[cc]
            )
            copy.start()
            copies.append(copy)
        return copies

    small[0].wait()
    passed = False
    for event in schedule():
        if event[0] == "s" and event[1] == 0:
            c = event[2]
            start_event(c)
            if not passed:
                pl.semaphore_wait(barrier, LEVELS + N_ORDER - 1)
                small[1].wait()
                passed = True
            level_copy(0, c).start()
            all_loads[c][2].wait()
            own_terms(0, c)
        elif event[0] == "s":
            _, k, c = event
            level_event(k - 1, c)
            if k < LEVELS:
                level_copy(k, c).start()
                own_terms(k, c)
        elif event[0] == "a":
            a2a_event(event[1])
        elif event[0] == "p":
            prepare_perm()
            prepare_pick()
        else:
            root_event(event[1])
    out_copies = finish()
    for k in range(LEVELS):
        for c in range(CHUNKS):
            level_copy(k, c).wait_send()
    for g in range(GROUPS):
        a2a_all(g).wait_send()
    for copy in out_copies:
        copy.wait()


def per_device(
    fourier, quad_weights, leaf_basis, level_factors, sparsity, root_basis, order_of_slot
):
    anywhere = pl.BlockSpec(memory_space=pl.ANY)
    vmem = pltpu.VMEM
    return pl.pallas_call(
        kernel,
        out_shape=jax.ShapeDtypeStruct((2, 2, 128, 512), BF16),
        in_specs=[anywhere] * 7,
        out_specs=anywhere,
        scratch_shapes=[
            vmem((SLOTS, 64, 128), BF16),
            vmem((1, 128), F32),
            vmem((SLOTS, 64, 128), BF16),
            vmem((SLOTS, LEVELS, 2, 64, 64), BF16),
            pltpu.SMEM((LEVELS, 1, SLOTS), I32),
            vmem((512, 64, 128), BF16),
            vmem((4, 128), I32),
            vmem((2, 2, 128, 512), BF16),
            vmem((LEVELS + 1, CHUNKS, 2, RANK, 128), BF16),
            vmem((LEVELS, CHUNKS, 2, RANK, 128), BF16),
            vmem((LEVELS, CHUNKS, 2, RANK, 128), F32),
            vmem((256, 256), BF16),
            vmem((GROUPS, N_ORDER, 16, 128), BF16),
            vmem((GROUPS, N_ORDER, 16, 128), BF16),
            vmem((512, 128), F32),
            vmem((512, 512), BF16),
            vmem((512, 128), F32),
            vmem((4, 128, 512), BF16),
            pltpu.SemaphoreType.DMA((3, CHUNKS)),
            pltpu.SemaphoreType.DMA((3,)),
            pltpu.SemaphoreType.DMA,
            pltpu.SemaphoreType.DMA((4,)),
            pltpu.SemaphoreType.DMA((LEVELS, CHUNKS)),
            pltpu.SemaphoreType.DMA((LEVELS, CHUNKS)),
            pltpu.SemaphoreType.DMA((GROUPS,)),
            pltpu.SemaphoreType.DMA((GROUPS,)),
        ],
        compiler_params=pltpu.CompilerParams(
            collective_id=0, has_side_effects=True, vmem_limit_bytes=60 * 1024 * 1024
        ),
        cost_estimate=pl.CostEstimate(
            flops=2 * 10**9, bytes_accessed=15 * 10**6, transcendentals=0
        ),
    )(
        fourier,
        quad_weights.reshape(1, 128),
        leaf_basis,
        level_factors,
        sparsity.transpose(1, 2, 0),
        root_basis,
        order_of_slot.reshape(4, 128),
    )


def solution(mesh):
    return jax.shard_map(
        per_device,
        mesh=mesh,
        in_specs=(
            P("order", None, "lat"),
            P("lat"),
            P("order", None, "lat"),
            P("order", None, None, "lat", None, None),
            P("order", None, "lat"),
            P(None, None, "lat"),
            P(),
        ),
        out_specs=P("order", None, "lat", None),
        check_vma=False,
    )
```

```python
import functools

import jax
import jax.numpy as jnp
from jax import lax
from jax.experimental import pallas as pl
from jax.experimental.pallas import tpu as pltpu
from jax.sharding import PartitionSpec as P

DEGREES = 2048
MESH = pl.DeviceIdType.MESH
BF16 = jnp.bfloat16
F32 = jnp.float32
I32 = jnp.int32

SLOTS = 32
CHUNK = 4
CHUNKS = SLOTS // CHUNK
LEVELS = 4
GROUPS = ((0, 1), (2, 3), (4, 5), (6,), (7,))
LAST = len(GROUPS) - 1
N_ORDER = 16
RANK = 64


HOPS = [(0, 1, 2, 1)[k >> 2] + (0, 1, 2, 1)[k & 3] for k in range(N_ORDER)]
NEAR = [k for k in range(1, N_ORDER) if HOPS[k] <= 2]
FAR = [k for k in range(1, N_ORDER) if HOPS[k] > 2]


def schedule():
    keyed = []
    for c in range(CHUNKS):
        keyed.append((c * 1.0, 0, ("s", 0, c)))
        keyed.append((c * 1.0 + 2.5, 1, ("s", 1, c)))
        keyed.append((c * 2.0 + 5.5, 2, ("s", 2, c)))
        keyed.append((c * 2.0 + 13.6, 3, ("s", 3, c)))
        keyed.append((c * 2.0 + 21.7, 4, ("s", 4, c)))
    for g, chunks in enumerate(GROUPS):
        keyed.append((chunks[-1] * 2.0 + 21.8, 5, ("a", g)))
        keyed.append((999 + g, 6, ("r", g)))
    keyed.append((8.1, 7, ("p",)))
    return [event for _, _, event in sorted(keyed)]


def kernel(
    four_hbm, quad_hbm, leaf_hbm, fac_hbm, spars_hbm, root_hbm, order_hbm, coef_hbm, pick_hbm,
    four, quad, leaf, fac, spars, root, order,
    state, partner, own, perm, send_buf, recv_buf, order_col, pick, coef, coef_t,
    in_sem, small_sem, root_sem, out_sem, send_sem, recv_sem, a2a_send_sem, a2a_recv_sem,
):
    me_o = lax.axis_index("order")
    me_l = lax.axis_index("lat")
    peers = [me_l ^ (1 << k) for k in range(LEVELS)]

    def loads(c):
        span = pl.ds(c * CHUNK, CHUNK)
        return [
            pltpu.make_async_copy(four_hbm.at[span], four.at[span], in_sem.at[0, c]),
            pltpu.make_async_copy(leaf_hbm.at[span], leaf.at[span], in_sem.at[1, c]),
            pltpu.make_async_copy(fac_hbm.at[span, :, :, 0], fac.at[span], in_sem.at[2, c]),
        ]

    small = [
        pltpu.make_async_copy(quad_hbm, quad, small_sem.at[0]),
        pltpu.make_async_copy(spars_hbm, spars, small_sem.at[1]),
        pltpu.make_async_copy(order_hbm, order, small_sem.at[2]),
    ]
    root_copy = pltpu.make_async_copy(root_hbm, root, root_sem)
    all_loads = [loads(c) for c in range(CHUNKS)]
    for copy in small:
        copy.start()
    for c in range(CHUNKS):
        for copy in all_loads[c]:
            copy.start()
    root_copy.start()

    barrier = pltpu.get_barrier_semaphore()
    for peer in peers:
        pl.semaphore_signal(barrier, inc=1, device_id=(me_o, peer), device_id_type=MESH)
    for i in range(1, N_ORDER):
        pl.semaphore_signal(
            barrier, inc=1, device_id=(lax.rem(me_o + i, N_ORDER), me_l), device_id_type=MESH
        )

    def level_copy(k, c):
        return pltpu.make_async_remote_copy(
            src_ref=state.at[k, c],
            dst_ref=partner.at[k, c],
            send_sem=send_sem.at[k, c],
            recv_sem=recv_sem.at[k, c],
            device_id=(me_o, peers[k]),
            device_id_type=MESH,
        )

    def a2a_copy(g, k):
        return pltpu.make_async_remote_copy(
            src_ref=send_buf.at[g, me_o ^ k],
            dst_ref=recv_buf.at[g, k],
            send_sem=a2a_send_sem.at[g],
            recv_sem=a2a_recv_sem.at[g, int(g == LAST and k in FAR)],
            device_id=(me_o ^ k, me_l),
            device_id_type=MESH,
        )

    def a2a_bytes(g, count, far=0):
        return pltpu.make_async_remote_copy(
            src_ref=send_buf.at[g, pl.ds(0, count)],
            dst_ref=recv_buf.at[g, pl.ds(0, count)],
            send_sem=a2a_send_sem.at[g],
            recv_sem=a2a_recv_sem.at[g, far],
            device_id=(me_o ^ 1, me_l),
            device_id_type=MESH,
        )

    low = lax.broadcasted_iota(I32, (RANK, 128), 1) < RANK

    def both(a, b):
        return jnp.concatenate([a, b], axis=0)

    def diagonal(product):
        return jnp.where(low, product[:RANK], product[RANK:])

    def own_terms(k, c):
        for h in range(2):
            s0, s1 = c * CHUNK + h, c * CHUNK + 2 + h
            a = both(fac[s0, k, 0], fac[s1, k, 0])
            own[k, c, h] = diagonal(jnp.dot(a, state[k, c, h], preferred_element_type=F32))

    def start_event(c):
        for copy in all_loads[c][:2]:
            copy.wait()
        w = quad[...]
        for h in range(2):
            s0, s1 = c * CHUNK + h, c * CHUNK + 2 + h
            weighted = both(
                (four[s0].astype(F32) * w).astype(BF16), (four[s1].astype(F32) * w).astype(BF16)
            )
            basis = both(leaf[s0], leaf[s1])
            product = lax.dot_general(
                basis, weighted, (((1,), (1,)), ((), ())), preferred_element_type=F32
            )
            state[0, c, h] = diagonal(product).astype(BF16)

    def level_event(k, c):
        level_copy(k, c).wait_recv()
        for h in range(2):
            s0, s1 = c * CHUNK + h, c * CHUNK + 2 + h
            b = both(fac[s0, k, 1], fac[s1, k, 1])
            cross = diagonal(jnp.dot(b, partner[k, c, h], preferred_element_type=F32))
            present = jnp.where(low, spars[k, 0, s0], spars[k, 0, s1]).astype(F32)
            state[k + 1, c, h] = (own[k, c, h] + present * cross).astype(BF16)

    def a2a_event(g):
        x = [state[LEVELS, c].reshape(2 * RANK, 128) for c in GROUPS[g]]
        packed = lax.dot_general(
            perm[:, : 128 * len(x)],
            jnp.concatenate(x, axis=1),
            (((1,), (1,)), ((), ())),
            preferred_element_type=F32,
        ).astype(BF16)
        send_buf[g] = packed.reshape(N_ORDER, 16, 128)
        for k in sorted(NEAR + FAR, key=lambda k: -HOPS[k]):
            a2a_copy(g, k).start()
        recv_buf[g, 0] = send_buf[g, me_o]

    def prepare_perm():
        row = lax.broadcasted_iota(I32, (256, 256), 0)
        col = lax.broadcasted_iota(I32, (256, 256), 1)
        target = (row & 3) * 64 + (row >> 4) * 4 + ((row >> 2) & 3)
        perm[...] = (col == target).astype(F32).astype(BF16)

    def prepare_pick():
        small[2].wait()
        orders = order[...].astype(F32)
        for i in range(4):
            wide = jnp.broadcast_to(orders[i : i + 1], (128, 128))
            order_col[pl.ds(i * 128, 128)] = wide.T
        window = lax.broadcasted_iota(I32, (16, 512), 1).astype(F32)
        for g in range(SLOTS // 8):
            for q in range(4):
                for h in range(2):
                    col = order_col[pl.ds(8 * g + 2 * q + h, 16, stride=SLOTS), :]
                    wide = jnp.concatenate([col] * 4, axis=1)
                    row = g * 128 + q * 32 + h * 16
                    pick[pl.ds(row, 16)] = (wide == window).astype(F32).astype(BF16)
        pick_copy.start()

    def root_event(g):
        if g == 0:
            root_copy.wait()
        pair = len(GROUPS[g]) == 2
        row = lax.broadcasted_iota(I32, (32, 256), 0)
        col = lax.broadcasted_iota(I32, (32, 256), 1)
        keep = ((row >> 4) == ((col >> 6) & 1)) & ((row & 1) == (col >> 7))
        keep = keep.astype(F32).astype(BF16)
        first = (lax.broadcasted_iota(I32, (32, 128), 0) & 2) == 0

        def one(k):
            source = me_o ^ k
            r = recv_buf[g, k]
            r2 = jnp.concatenate([r, r], axis=1)
            lhs = jnp.concatenate([r2, r2], axis=0) * keep
            base = source * SLOTS + GROUPS[g][0] * CHUNK
            w = root[pl.ds(base, 4)].reshape(256, 128)
            if pair:
                w = jnp.concatenate([w, root[pl.ds(base + 4, 4)].reshape(256, 128)], axis=1)
            product = jnp.dot(lhs, w, preferred_element_type=F32)
            if pair:
                product = jnp.where(first, product[:, :128], product[:, 128:])
            coef[pl.ds(pl.multiple_of(source * 32, 32), 32)] = product

        if g == LAST:
            one(0)
            a2a_bytes(g, len(NEAR), 0).wait_recv()
            for k in NEAR:
                one(k)
            a2a_bytes(g, len(FAR), 1).wait_recv()
            for k in FAR:
                one(k)
        else:
            a2a_bytes(g, N_ORDER - 1).wait_recv()

            def body(k, carry):
                one(k)
                return carry

            lax.fori_loop(0, N_ORDER, body, 0, unroll=4)
        width = 128 if pair else 64
        lanes = pl.ds(GROUPS[g][0] * 64, width)
        for cc in range(4):
            parts = []
            for q in range(width // 32):
                for h in range(2):
                    parts.append(coef[pl.ds(h * 16 + cc * 4 + q, 16, stride=32), :])
            coef_t[cc, :, lanes] = jnp.concatenate(parts, axis=0).T.astype(BF16)
        if pair or g == LAST:
            coef_copy(g if pair else 3).start()

    def coef_copy(block):
        lanes = pl.ds(block * 128, 128)
        return pltpu.make_async_copy(
            coef_t.at[:, :, lanes], coef_hbm.at[:, :, lanes], out_sem.at[block]
        )

    pick_copy = pltpu.make_async_copy(pick, pick_hbm, out_sem.at[4])

    small[0].wait()
    passed = False
    for event in schedule():
        if event[0] == "s" and event[1] == 0:
            c = event[2]
            start_event(c)
            if not passed:
                pl.semaphore_wait(barrier, LEVELS + N_ORDER - 1)
                small[1].wait()
                passed = True
            level_copy(0, c).start()
            all_loads[c][2].wait()
            own_terms(0, c)
        elif event[0] == "s":
            _, k, c = event
            level_event(k - 1, c)
            if k < LEVELS:
                level_copy(k, c).start()
                own_terms(k, c)
        elif event[0] == "a":
            a2a_event(event[1])
        elif event[0] == "p":
            prepare_perm()
            prepare_pick()
        else:
            root_event(event[1])
    for k in range(LEVELS):
        for c in range(CHUNKS):
            level_copy(k, c).wait_send()
    for g in range(len(GROUPS)):
        a2a_bytes(g, N_ORDER - 1).wait_send()
    pick_copy.wait()
    for block in range(4):
        coef_copy(block).wait()


def finish_kernel(coef_hbm, pick_hbm, out_hbm, coef_t, pick, out, in_sem, out_sem):
    pick_copy = pltpu.make_async_copy(pick_hbm, pick, in_sem.at[4])
    coef_copies = [
        pltpu.make_async_copy(coef_hbm.at[cc], coef_t.at[cc], in_sem.at[cc]) for cc in range(4)
    ]
    pick_copy.start()
    for copy in coef_copies:
        copy.start()
    degree = lax.axis_index("lat") * 128 + lax.broadcasted_iota(I32, (128, 512), 0)
    window = DEGREES // 512 * lax.broadcasted_iota(I32, (128, 512), 1)
    alive = degree >= window
    pick_copy.wait()
    out_copies = []
    for cc in range(4):
        coef_copies[cc].wait()
        natural = jnp.dot(coef_t[cc], pick[...], preferred_element_type=F32)
        out[cc] = jnp.where(alive, natural, 0.0).astype(BF16)
        copy = pltpu.make_async_copy(out.at[cc], out_hbm.at[cc // 2, cc % 2], out_sem.at[cc])
        copy.start()
        out_copies.append(copy)
    for copy in out_copies:
        copy.wait()


def per_device(
    fourier, quad_weights, leaf_basis, level_factors, sparsity, root_basis, order_of_slot
):
    anywhere = pl.BlockSpec(memory_space=pl.ANY)
    vmem = pltpu.VMEM
    coef, pick = pl.pallas_call(
        kernel,
        out_shape=[
            jax.ShapeDtypeStruct((4, 128, 512), BF16),
            jax.ShapeDtypeStruct((512, 512), BF16),
        ],
        in_specs=[anywhere] * 7,
        out_specs=[anywhere] * 2,
        scratch_shapes=[
            vmem((SLOTS, 64, 128), BF16),
            vmem((1, 128), F32),
            vmem((SLOTS, 64, 128), BF16),
            vmem((SLOTS, LEVELS, 2, 64, 64), BF16),
            pltpu.SMEM((LEVELS, 1, SLOTS), I32),
            vmem((512, 64, 128), BF16),
            vmem((4, 128), I32),
            vmem((LEVELS + 1, CHUNKS, 2, RANK, 128), BF16),
            vmem((LEVELS, CHUNKS, 2, RANK, 128), BF16),
            vmem((LEVELS, CHUNKS, 2, RANK, 128), F32),
            vmem((256, 256), BF16),
            vmem((len(GROUPS), N_ORDER, 16, 128), BF16),
            vmem((len(GROUPS), N_ORDER, 16, 128), BF16),
            vmem((512, 128), F32),
            vmem((512, 512), BF16),
            vmem((512, 128), F32),
            vmem((4, 128, 512), BF16),
            pltpu.SemaphoreType.DMA((3, CHUNKS)),
            pltpu.SemaphoreType.DMA((3,)),
            pltpu.SemaphoreType.DMA,
            pltpu.SemaphoreType.DMA((5,)),
            pltpu.SemaphoreType.DMA((LEVELS, CHUNKS)),
            pltpu.SemaphoreType.DMA((LEVELS, CHUNKS)),
            pltpu.SemaphoreType.DMA((len(GROUPS),)),
            pltpu.SemaphoreType.DMA((len(GROUPS), 2)),
        ],
        compiler_params=pltpu.CompilerParams(
            collective_id=0, has_side_effects=True, vmem_limit_bytes=60 * 1024 * 1024
        ),
        cost_estimate=pl.CostEstimate(
            flops=2 * 10**9, bytes_accessed=15 * 10**6, transcendentals=0
        ),
    )(
        fourier,
        quad_weights.reshape(1, 128),
        leaf_basis,
        level_factors,
        sparsity.transpose(1, 2, 0),
        root_basis,
        order_of_slot.reshape(4, 128),
    )
    return pl.pallas_call(
        finish_kernel,
        out_shape=jax.ShapeDtypeStruct((2, 2, 128, 512), BF16),
        in_specs=[anywhere] * 2,
        out_specs=anywhere,
        scratch_shapes=[
            vmem((4, 128, 512), BF16),
            vmem((512, 512), BF16),
            vmem((4, 128, 512), BF16),
            pltpu.SemaphoreType.DMA((5,)),
            pltpu.SemaphoreType.DMA((4,)),
        ],
        compiler_params=pltpu.CompilerParams(vmem_limit_bytes=60 * 1024 * 1024),
        cost_estimate=pl.CostEstimate(
            flops=2 * 512**3, bytes_accessed=3 * 2**19, transcendentals=0
        ),
    )(coef, pick)


def solution(mesh):
    return jax.shard_map(
        per_device,
        mesh=mesh,
        in_specs=(
            P("order", None, "lat"),
            P("lat"),
            P("order", None, "lat"),
            P("order", None, None, "lat", None, None),
            P("order", None, "lat"),
            P(None, None, "lat"),
            P(),
        ),
        out_specs=P("order", None, "lat", None),
        check_vma=False,
    )
```

```python
import functools

import jax
import jax.numpy as jnp
from jax import lax
from jax.experimental import pallas as pl
from jax.experimental.pallas import tpu as pltpu
from jax.sharding import PartitionSpec as P

DEGREES = 2048
MESH = pl.DeviceIdType.MESH
BF16 = jnp.bfloat16
F32 = jnp.float32
I32 = jnp.int32

SLOTS = 32
CHUNK = 4
CHUNKS = SLOTS // CHUNK
LEVELS = 4
GROUPS = ((0, 1), (2, 3), (4, 5), (6,), (7,))
LAST = len(GROUPS) - 1
N_ORDER = 16
RANK = 64


HOPS = [(0, 1, 2, 1)[k >> 2] + (0, 1, 2, 1)[k & 3] for k in range(N_ORDER)]
NEAR = [k for k in range(1, N_ORDER) if HOPS[k] <= 2]
FAR = [k for k in range(1, N_ORDER) if HOPS[k] > 2]


def schedule():
    keyed = []
    for c in range(CHUNKS):
        keyed.append((c * 1.0, 0, ("s", 0, c)))
        keyed.append((c * 1.0 + 2.5, 1, ("s", 1, c)))
        keyed.append((c * 1.0 + 5.5, 2, ("s", 2, c)))
        keyed.append((c * 2.0 + 12.0, 3, ("s", 3, c)))
        keyed.append((c * 2.0 + 18.5, 4, ("s", 4, c)))
    for g, chunks in enumerate(GROUPS):
        keyed.append((chunks[-1] * 2.0 + 18.6, 5, ("a", g)))
        keyed.append((999 + g, 6, ("r", g)))
    keyed.append((8.1, 7, ("p",)))
    return [event for _, _, event in sorted(keyed)]


def kernel(
    four_hbm, quad_hbm, leaf_hbm, fac_hbm, spars_hbm, root_hbm, order_hbm, part_hbm, coef_hbm, pick_hbm,
    four, quad, leaf, fac, spars, root, order,
    state, partner, own, perm, send_buf, recv_buf, order_col, pick, coef, coef_t, part,
    in_sem, small_sem, root_sem, out_sem, send_sem, recv_sem, a2a_send_sem, a2a_recv_sem,
):
    me_o = lax.axis_index("order")
    me_l = lax.axis_index("lat")
    peers = [me_l ^ (1 << k) for k in range(LEVELS)]

    def loads(c):
        span = pl.ds(c * CHUNK, CHUNK)
        return [
            pltpu.make_async_copy(four_hbm.at[span], four.at[span], in_sem.at[0, c]),
            pltpu.make_async_copy(leaf_hbm.at[span], leaf.at[span], in_sem.at[1, c]),
            pltpu.make_async_copy(fac_hbm.at[span, :, :, 0], fac.at[span], in_sem.at[2, c]),
        ]

    small = [
        pltpu.make_async_copy(quad_hbm, quad, small_sem.at[0]),
        pltpu.make_async_copy(spars_hbm, spars, small_sem.at[1]),
        pltpu.make_async_copy(order_hbm, order, small_sem.at[2]),
    ]
    root_copy = pltpu.make_async_copy(root_hbm, root, root_sem)
    all_loads = [loads(c) for c in range(CHUNKS)]
    for copy in (all_loads[0][0], all_loads[0][1], small[0]):
        copy.start()

    barrier = pltpu.get_barrier_semaphore()
    for peer in peers:
        pl.semaphore_signal(barrier, inc=1, device_id=(me_o, peer), device_id_type=MESH)
    for i in range(1, N_ORDER):
        pl.semaphore_signal(
            barrier, inc=1, device_id=(lax.rem(me_o + i, N_ORDER), me_l), device_id_type=MESH
        )

    for c in range(1, CHUNKS):
        for copy in all_loads[c][:2]:
            copy.start()
    for copy in small[1:]:
        copy.start()
    for c in range(CHUNKS):
        all_loads[c][2].start()

    def level_copy(k, c):
        return pltpu.make_async_remote_copy(
            src_ref=state.at[k, c],
            dst_ref=partner.at[k, c],
            send_sem=send_sem.at[k, c],
            recv_sem=recv_sem.at[k, c],
            device_id=(me_o, peers[k]),
            device_id_type=MESH,
        )

    def a2a_copy(g, k):
        return pltpu.make_async_remote_copy(
            src_ref=send_buf.at[g, me_o ^ k],
            dst_ref=recv_buf.at[g, k],
            send_sem=a2a_send_sem.at[g],
            recv_sem=a2a_recv_sem.at[g, int(g == LAST and k in FAR)],
            device_id=(me_o ^ k, me_l),
            device_id_type=MESH,
        )

    def a2a_bytes(g, count, far=0):
        return pltpu.make_async_remote_copy(
            src_ref=send_buf.at[g, pl.ds(0, count)],
            dst_ref=recv_buf.at[g, pl.ds(0, count)],
            send_sem=a2a_send_sem.at[g],
            recv_sem=a2a_recv_sem.at[g, far],
            device_id=(me_o ^ 1, me_l),
            device_id_type=MESH,
        )

    low = lax.broadcasted_iota(I32, (RANK, 128), 1) < RANK

    def both(a, b):
        return jnp.concatenate([a, b], axis=0)

    def diagonal(product):
        return jnp.where(low, product[:RANK], product[RANK:])

    def own_terms(k, c):
        for h in range(2):
            s0, s1 = c * CHUNK + h, c * CHUNK + 2 + h
            a = both(fac[s0, k, 0], fac[s1, k, 0])
            own[k, c, h] = diagonal(jnp.dot(a, state[k, c, h], preferred_element_type=F32))

    def start_event(c):
        for copy in all_loads[c][:2]:
            copy.wait()
        w = quad[...]
        for h in range(2):
            s0, s1 = c * CHUNK + h, c * CHUNK + 2 + h
            weighted = both(
                (four[s0].astype(F32) * w).astype(BF16), (four[s1].astype(F32) * w).astype(BF16)
            )
            basis = both(leaf[s0], leaf[s1])
            product = lax.dot_general(
                basis, weighted, (((1,), (1,)), ((), ())), preferred_element_type=F32
            )
            state[0, c, h] = diagonal(product).astype(BF16)

    def level_event(k, c):
        level_copy(k, c).wait_recv()
        for h in range(2):
            s0, s1 = c * CHUNK + h, c * CHUNK + 2 + h
            b = both(fac[s0, k, 1], fac[s1, k, 1])
            cross = diagonal(jnp.dot(b, partner[k, c, h], preferred_element_type=F32))
            present = jnp.where(low, spars[k, 0, s0], spars[k, 0, s1]).astype(F32)
            state[k + 1, c, h] = (own[k, c, h] + present * cross).astype(BF16)

    def a2a_event(g):
        x = [state[LEVELS, c].reshape(2 * RANK, 128) for c in GROUPS[g]]
        packed = lax.dot_general(
            perm[:, : 128 * len(x)],
            jnp.concatenate(x, axis=1),
            (((1,), (1,)), ((), ())),
            preferred_element_type=F32,
        ).astype(BF16)
        send_buf[g] = packed.reshape(N_ORDER, 16, 128)
        for k in sorted(NEAR + FAR, key=lambda k: -HOPS[k]):
            a2a_copy(g, k).start()
        recv_buf[g, 0] = send_buf[g, me_o]

    def prepare_perm():
        row = lax.broadcasted_iota(I32, (256, 256), 0)
        col = lax.broadcasted_iota(I32, (256, 256), 1)
        target = (row & 3) * 64 + (row >> 4) * 4 + ((row >> 2) & 3)
        perm[...] = (col == target).astype(F32).astype(BF16)

    def prepare_pick():
        small[2].wait()
        orders = order[...].astype(F32)
        for i in range(4):
            wide = jnp.broadcast_to(orders[i : i + 1], (128, 128))
            order_col[pl.ds(i * 128, 128)] = wide.T
        window = lax.broadcasted_iota(I32, (16, 512), 1).astype(F32)
        for g in range(SLOTS // 8):
            for q in range(4):
                for h in range(2):
                    col = order_col[pl.ds(8 * g + 2 * q + h, 16, stride=SLOTS), :]
                    wide = jnp.concatenate([col] * 4, axis=1)
                    row = g * 128 + q * 32 + h * 16
                    pick[pl.ds(row, 16)] = (wide == window).astype(F32).astype(BF16)
        pick_copy.start()

    def root_event(g):
        if g == 0:
            root_copy.wait()
        pair = len(GROUPS[g]) == 2
        row = lax.broadcasted_iota(I32, (32, 256), 0)
        col = lax.broadcasted_iota(I32, (32, 256), 1)
        keep = ((row >> 4) == ((col >> 6) & 1)) & ((row & 1) == (col >> 7))
        keep = keep.astype(F32).astype(BF16)
        first = (lax.broadcasted_iota(I32, (32, 128), 0) & 2) == 0

        def one(k):
            source = me_o ^ k
            r = recv_buf[g, k]
            r2 = jnp.concatenate([r, r], axis=1)
            lhs = jnp.concatenate([r2, r2], axis=0) * keep
            base = source * SLOTS + GROUPS[g][0] * CHUNK
            w = root[pl.ds(base, 4)].reshape(256, 128)
            if pair:
                w = jnp.concatenate([w, root[pl.ds(base + 4, 4)].reshape(256, 128)], axis=1)
            product = jnp.dot(lhs, w, preferred_element_type=F32)
            if pair:
                product = jnp.where(first, product[:, :128], product[:, 128:])
            coef[pl.ds(pl.multiple_of(source * 32, 32), 32)] = product

        if g == LAST:
            one(0)
            a2a_bytes(g, len(NEAR), 0).wait_recv()
            for k in NEAR:
                one(k)
            a2a_bytes(g, len(FAR), 1).wait_recv()
            for k in FAR:
                one(k)
        else:
            a2a_bytes(g, N_ORDER - 1).wait_recv()

            def body(k, carry):
                one(k)
                return carry

            lax.fori_loop(0, N_ORDER, body, 0, unroll=4)
        width = 128 if pair else 64
        lanes = pl.ds(GROUPS[g][0] * 64, width)
        for cc in range(4):
            parts = []
            for q in range(width // 32):
                for h in range(2):
                    parts.append(coef[pl.ds(h * 16 + cc * 4 + q, 16, stride=32), :])
            coef_t[cc, :, lanes] = jnp.concatenate(parts, axis=0).T.astype(BF16)
        if g == 2:
            part[...] = jnp.dot(
                coef_t[:, :, :384].reshape(512, 384), pick[:384], preferred_element_type=F32
            ).astype(BF16)
            part_copy.start()
        if g == LAST:
            coef_copy.start()

    coef_copy = pltpu.make_async_copy(coef_t.at[:, :, pl.ds(384, 128)], coef_hbm, out_sem.at[0])
    pick_copy = pltpu.make_async_copy(pick.at[pl.ds(384, 128)], pick_hbm, out_sem.at[1])
    part_copy = pltpu.make_async_copy(part, part_hbm, out_sem.at[2])

    small[0].wait()
    passed = False
    for event in schedule():
        if event[0] == "s" and event[1] == 0:
            c = event[2]
            start_event(c)
            if not passed:
                pl.semaphore_wait(barrier, LEVELS + N_ORDER - 1)
                passed = True
            level_copy(0, c).start()
        elif event[0] == "s":
            _, k, c = event
            if event == ("s", 1, 0):
                small[1].wait()
            if k == 1:
                all_loads[c][2].wait()
                own_terms(0, c)
            level_event(k - 1, c)
            if k < LEVELS:
                level_copy(k, c).start()
                own_terms(k, c)
        elif event[0] == "a":
            a2a_event(event[1])
        elif event[0] == "p":
            root_copy.start()
            prepare_perm()
            prepare_pick()
        else:
            root_event(event[1])
    for k in range(LEVELS):
        for c in range(CHUNKS):
            level_copy(k, c).wait_send()
    for g in range(len(GROUPS)):
        a2a_bytes(g, N_ORDER - 1).wait_send()
    for copy in (pick_copy, part_copy, coef_copy):
        copy.wait()


def finish_kernel(part_hbm, coef_hbm, pick_hbm, out_hbm, part, coef_t, pick, out, in_sem, out_sem):
    copies = [
        pltpu.make_async_copy(coef_hbm, coef_t, in_sem.at[0]),
        pltpu.make_async_copy(pick_hbm, pick, in_sem.at[1]),
        pltpu.make_async_copy(part_hbm, part, in_sem.at[2]),
    ]
    for copy in copies:
        copy.start()
    degree = lax.axis_index("lat") * 128 + lax.broadcasted_iota(I32, (128, 512), 0)
    window = DEGREES // 512 * lax.broadcasted_iota(I32, (128, 512), 1)
    alive = degree >= window
    for copy in copies:
        copy.wait()
    natural = jnp.dot(coef_t[...].reshape(512, 128), pick[...], preferred_element_type=F32)
    out_copies = []
    for cc in range(4):
        rows = slice(cc * 128, (cc + 1) * 128)
        total = part[rows].astype(F32) + natural[rows]
        out[cc] = jnp.where(alive, total, 0.0).astype(BF16)
        copy = pltpu.make_async_copy(out.at[cc], out_hbm.at[cc // 2, cc % 2], out_sem.at[cc])
        copy.start()
        out_copies.append(copy)
    for copy in out_copies:
        copy.wait()


def per_device(
    fourier, quad_weights, leaf_basis, level_factors, sparsity, root_basis, order_of_slot
):
    anywhere = pl.BlockSpec(memory_space=pl.ANY)
    vmem = pltpu.VMEM
    parts = pl.pallas_call(
        kernel,
        out_shape=[
            jax.ShapeDtypeStruct((512, 512), BF16),
            jax.ShapeDtypeStruct((4, 128, 128), BF16),
            jax.ShapeDtypeStruct((128, 512), BF16),
        ],
        in_specs=[anywhere] * 7,
        out_specs=[anywhere] * 3,
        scratch_shapes=[
            vmem((SLOTS, 64, 128), BF16),
            vmem((1, 128), F32),
            vmem((SLOTS, 64, 128), BF16),
            vmem((SLOTS, LEVELS, 2, 64, 64), BF16),
            pltpu.SMEM((LEVELS, 1, SLOTS), I32),
            vmem((512, 64, 128), BF16),
            vmem((4, 128), I32),
            vmem((LEVELS + 1, CHUNKS, 2, RANK, 128), BF16),
            vmem((LEVELS, CHUNKS, 2, RANK, 128), BF16),
            vmem((LEVELS, CHUNKS, 2, RANK, 128), F32),
            vmem((256, 256), BF16),
            vmem((len(GROUPS), N_ORDER, 16, 128), BF16),
            vmem((len(GROUPS), N_ORDER, 16, 128), BF16),
            vmem((512, 128), F32),
            vmem((512, 512), BF16),
            vmem((512, 128), F32),
            vmem((4, 128, 512), BF16),
            vmem((512, 512), BF16),
            pltpu.SemaphoreType.DMA((3, CHUNKS)),
            pltpu.SemaphoreType.DMA((3,)),
            pltpu.SemaphoreType.DMA,
            pltpu.SemaphoreType.DMA((3,)),
            pltpu.SemaphoreType.DMA((LEVELS, CHUNKS)),
            pltpu.SemaphoreType.DMA((LEVELS, CHUNKS)),
            pltpu.SemaphoreType.DMA((len(GROUPS),)),
            pltpu.SemaphoreType.DMA((len(GROUPS), 2)),
        ],
        compiler_params=pltpu.CompilerParams(
            collective_id=0, has_side_effects=True, vmem_limit_bytes=60 * 1024 * 1024
        ),
        cost_estimate=pl.CostEstimate(
            flops=2 * 10**9, bytes_accessed=15 * 10**6, transcendentals=0
        ),
    )(
        fourier,
        quad_weights.reshape(1, 128),
        leaf_basis,
        level_factors,
        sparsity.transpose(1, 2, 0),
        root_basis,
        order_of_slot.reshape(4, 128),
    )
    return pl.pallas_call(
        finish_kernel,
        out_shape=jax.ShapeDtypeStruct((2, 2, 128, 512), BF16),
        in_specs=[anywhere] * 3,
        out_specs=anywhere,
        scratch_shapes=[
            vmem((512, 512), BF16),
            vmem((4, 128, 128), BF16),
            vmem((128, 512), BF16),
            vmem((4, 128, 512), BF16),
            pltpu.SemaphoreType.DMA((3,)),
            pltpu.SemaphoreType.DMA((4,)),
        ],
        compiler_params=pltpu.CompilerParams(vmem_limit_bytes=60 * 1024 * 1024),
        cost_estimate=pl.CostEstimate(
            flops=2**26, bytes_accessed=5 * 2**18, transcendentals=0
        ),
    )(*parts)


def solution(mesh):
    return jax.shard_map(
        per_device,
        mesh=mesh,
        in_specs=(
            P("order", None, "lat"),
            P("lat"),
            P("order", None, "lat"),
            P("order", None, None, "lat", None, None),
            P("order", None, "lat"),
            P(None, None, "lat"),
            P(),
        ),
        out_specs=P("order", None, "lat", None),
        check_vma=False,
    )
```

```python
import functools

import jax
import jax.numpy as jnp
from jax import lax
from jax.experimental import pallas as pl
from jax.experimental.pallas import tpu as pltpu
from jax.sharding import PartitionSpec as P

DEGREES = 2048
MESH = pl.DeviceIdType.MESH
BF16 = jnp.bfloat16
F32 = jnp.float32
I32 = jnp.int32

SLOTS = 32
CHUNK = 4
CHUNKS = SLOTS // CHUNK
LEVELS = 4
GROUPS = ((0, 1), (2, 3), (4, 5), (6,), (7,))
LAST = len(GROUPS) - 1
N_ORDER = 16
RANK = 64


HOPS = [(0, 1, 2, 1)[k >> 2] + (0, 1, 2, 1)[k & 3] for k in range(N_ORDER)]
NEAR = [k for k in range(1, N_ORDER) if HOPS[k] <= 2]
FAR = [k for k in range(1, N_ORDER) if HOPS[k] > 2]


def schedule():
    keyed = []
    for c in range(CHUNKS):
        keyed.append((c * 1.0, 0, ("s", 0, c)))
        keyed.append((c * 1.0 + 2.5, 1, ("s", 1, c)))
        keyed.append((c * 1.0 + 5.5, 2, ("s", 2, c)))
        keyed.append((c * 2.0 + 12.0, 3, ("s", 3, c)))
        keyed.append((c * 2.0 + 18.5, 4, ("s", 4, c)))
    for g, chunks in enumerate(GROUPS):
        keyed.append((chunks[-1] * 2.0 + 18.6, 5, ("a", g)))
        keyed.append((999 + g, 6, ("r", g)))
    keyed.append((8.1, 7, ("p",)))
    return [event for _, _, event in sorted(keyed)]


ROUNDS = [("s", 1, 1), ("s", 2, 0), ("s", 3, 0)]


def kernel(
    four_hbm, quad_hbm, leaf_hbm, fac_hbm, spars_hbm, root_hbm, order_hbm, part_hbm, coef_hbm, pick_hbm,
    four, quad, leaf, fac, spars, root, order,
    state, partner, own, perm, send_buf, recv_buf, order_col, pick, coef, coef_t, part,
    in_sem, small_sem, root_sem, out_sem, send_sem, recv_sem, a2a_send_sem, a2a_recv_sem, round_sem,
):
    me_o = lax.axis_index("order")
    me_l = lax.axis_index("lat")
    peers = [me_l ^ (1 << k) for k in range(LEVELS)]

    def loads(c):
        span = pl.ds(c * CHUNK, CHUNK)
        return [
            pltpu.make_async_copy(four_hbm.at[span], four.at[span], in_sem.at[0, c]),
            pltpu.make_async_copy(leaf_hbm.at[span], leaf.at[span], in_sem.at[1, c]),
            pltpu.make_async_copy(fac_hbm.at[span, :, :, 0], fac.at[span], in_sem.at[2, c]),
        ]

    small = [
        pltpu.make_async_copy(quad_hbm, quad, small_sem.at[0]),
        pltpu.make_async_copy(spars_hbm, spars, small_sem.at[1]),
        pltpu.make_async_copy(order_hbm, order, small_sem.at[2]),
    ]
    root_copy = pltpu.make_async_copy(root_hbm, root, root_sem)
    all_loads = [loads(c) for c in range(CHUNKS)]
    for copy in (all_loads[0][0], all_loads[0][1], small[0]):
        copy.start()

    x, y = me_o // 4, lax.rem(me_o, 4)
    z, core = me_l // 2, lax.rem(me_l, 2)

    def around(axis):
        places = []
        for step in (1, -1):
            if axis == "x":
                places.append((lax.rem(x + step + 4, 4) * 4 + y, me_l))
            elif axis == "y":
                places.append((x * 4 + lax.rem(y + step + 4, 4), me_l))
            else:
                places.append((me_o, lax.rem(z + step + 8, 8) * 2 + core))
        return places

    barrier = pltpu.get_barrier_semaphore()
    neighbours = [(me_o, peers[0])] + around("x") + around("y") + around("z")
    for place in neighbours:
        pl.semaphore_signal(barrier, inc=1, device_id=place, device_id_type=MESH)

    def tell(n):
        for place in around("y" if n == 0 else "x") + around("z"):
            pl.semaphore_signal(round_sem.at[n], inc=1, device_id=place, device_id_type=MESH)

    def hear(n):
        pl.semaphore_wait(round_sem.at[n], 4)

    for c in range(1, CHUNKS):
        for copy in all_loads[c][:2]:
            copy.start()
    for copy in small[1:]:
        copy.start()
    for c in range(CHUNKS):
        all_loads[c][2].start()

    def level_copy(k, c):
        return pltpu.make_async_remote_copy(
            src_ref=state.at[k, c],
            dst_ref=partner.at[k, c],
            send_sem=send_sem.at[k, c],
            recv_sem=recv_sem.at[k, c],
            device_id=(me_o, peers[k]),
            device_id_type=MESH,
        )

    def a2a_copy(g, k):
        return pltpu.make_async_remote_copy(
            src_ref=send_buf.at[g, me_o ^ k],
            dst_ref=recv_buf.at[g, k],
            send_sem=a2a_send_sem.at[g],
            recv_sem=a2a_recv_sem.at[g, int(g == LAST and k in FAR)],
            device_id=(me_o ^ k, me_l),
            device_id_type=MESH,
        )

    def a2a_bytes(g, count, far=0):
        return pltpu.make_async_remote_copy(
            src_ref=send_buf.at[g, pl.ds(0, count)],
            dst_ref=recv_buf.at[g, pl.ds(0, count)],
            send_sem=a2a_send_sem.at[g],
            recv_sem=a2a_recv_sem.at[g, far],
            device_id=(me_o ^ 1, me_l),
            device_id_type=MESH,
        )

    low = lax.broadcasted_iota(I32, (RANK, 128), 1) < RANK

    def both(a, b):
        return jnp.concatenate([a, b], axis=0)

    def diagonal(product):
        return jnp.where(low, product[:RANK], product[RANK:])

    def own_terms(k, c):
        for h in range(2):
            s0, s1 = c * CHUNK + h, c * CHUNK + 2 + h
            a = both(fac[s0, k, 0], fac[s1, k, 0])
            own[k, c, h] = diagonal(jnp.dot(a, state[k, c, h], preferred_element_type=F32))

    def start_event(c):
        for copy in all_loads[c][:2]:
            copy.wait()
        w = quad[...]
        for h in range(2):
            s0, s1 = c * CHUNK + h, c * CHUNK + 2 + h
            weighted = both(
                (four[s0].astype(F32) * w).astype(BF16), (four[s1].astype(F32) * w).astype(BF16)
            )
            basis = both(leaf[s0], leaf[s1])
            product = lax.dot_general(
                basis, weighted, (((1,), (1,)), ((), ())), preferred_element_type=F32
            )
            state[0, c, h] = diagonal(product).astype(BF16)

    def level_event(k, c):
        level_copy(k, c).wait_recv()
        for h in range(2):
            s0, s1 = c * CHUNK + h, c * CHUNK + 2 + h
            b = both(fac[s0, k, 1], fac[s1, k, 1])
            cross = diagonal(jnp.dot(b, partner[k, c, h], preferred_element_type=F32))
            present = jnp.where(low, spars[k, 0, s0], spars[k, 0, s1]).astype(F32)
            state[k + 1, c, h] = (own[k, c, h] + present * cross).astype(BF16)

    def a2a_event(g):
        x = [state[LEVELS, c].reshape(2 * RANK, 128) for c in GROUPS[g]]
        packed = lax.dot_general(
            perm[:, : 128 * len(x)],
            jnp.concatenate(x, axis=1),
            (((1,), (1,)), ((), ())),
            preferred_element_type=F32,
        ).astype(BF16)
        send_buf[g] = packed.reshape(N_ORDER, 16, 128)
        for k in sorted(NEAR + FAR, key=lambda k: -HOPS[k]):
            a2a_copy(g, k).start()
        recv_buf[g, 0] = send_buf[g, me_o]

    def prepare_perm():
        row = lax.broadcasted_iota(I32, (256, 256), 0)
        col = lax.broadcasted_iota(I32, (256, 256), 1)
        target = (row & 3) * 64 + (row >> 4) * 4 + ((row >> 2) & 3)
        perm[...] = (col == target).astype(F32).astype(BF16)

    def prepare_pick():
        small[2].wait()
        orders = order[...].astype(F32)
        for i in range(4):
            wide = jnp.broadcast_to(orders[i : i + 1], (128, 128))
            order_col[pl.ds(i * 128, 128)] = wide.T
        window = lax.broadcasted_iota(I32, (16, 512), 1).astype(F32)
        for g in range(SLOTS // 8):
            for q in range(4):
                for h in range(2):
                    col = order_col[pl.ds(8 * g + 2 * q + h, 16, stride=SLOTS), :]
                    wide = jnp.concatenate([col] * 4, axis=1)
                    row = g * 128 + q * 32 + h * 16
                    pick[pl.ds(row, 16)] = (wide == window).astype(F32).astype(BF16)
        pick_copy.start()

    def root_event(g):
        if g == 0:
            root_copy.wait()
        pair = len(GROUPS[g]) == 2
        row = lax.broadcasted_iota(I32, (32, 256), 0)
        col = lax.broadcasted_iota(I32, (32, 256), 1)
        keep = ((row >> 4) == ((col >> 6) & 1)) & ((row & 1) == (col >> 7))
        keep = keep.astype(F32).astype(BF16)
        first = (lax.broadcasted_iota(I32, (32, 128), 0) & 2) == 0

        def one(k):
            source = me_o ^ k
            r = recv_buf[g, k]
            r2 = jnp.concatenate([r, r], axis=1)
            lhs = jnp.concatenate([r2, r2], axis=0) * keep
            base = source * SLOTS + GROUPS[g][0] * CHUNK
            w = root[pl.ds(base, 4)].reshape(256, 128)
            if pair:
                w = jnp.concatenate([w, root[pl.ds(base + 4, 4)].reshape(256, 128)], axis=1)
            product = jnp.dot(lhs, w, preferred_element_type=F32)
            if pair:
                product = jnp.where(first, product[:, :128], product[:, 128:])
            coef[pl.ds(pl.multiple_of(source * 32, 32), 32)] = product

        if g == LAST:
            one(0)
            a2a_bytes(g, len(NEAR), 0).wait_recv()
            for k in NEAR:
                one(k)
            a2a_bytes(g, len(FAR), 1).wait_recv()
            for k in FAR:
                one(k)
        else:
            a2a_bytes(g, N_ORDER - 1).wait_recv()

            def body(k, carry):
                one(k)
                return carry

            lax.fori_loop(0, N_ORDER, body, 0, unroll=4)
        width = 128 if pair else 64
        lanes = pl.ds(GROUPS[g][0] * 64, width)
        for cc in range(4):
            parts = []
            for q in range(width // 32):
                for h in range(2):
                    parts.append(coef[pl.ds(h * 16 + cc * 4 + q, 16, stride=32), :])
            coef_t[cc, :, lanes] = jnp.concatenate(parts, axis=0).T.astype(BF16)
        if g == 2:
            part[...] = jnp.dot(
                coef_t[:, :, :384].reshape(512, 384), pick[:384], preferred_element_type=F32
            ).astype(BF16)
            part_copy.start()
        if g == LAST:
            coef_copy.start()

    coef_copy = pltpu.make_async_copy(coef_t.at[:, :, pl.ds(384, 128)], coef_hbm, out_sem.at[0])
    pick_copy = pltpu.make_async_copy(pick.at[pl.ds(384, 128)], pick_hbm, out_sem.at[1])
    part_copy = pltpu.make_async_copy(part, part_hbm, out_sem.at[2])

    small[0].wait()
    passed = False
    for event in schedule():
        if event[0] == "s" and event[1] == 0:
            c = event[2]
            start_event(c)
            if not passed:
                pl.semaphore_wait(barrier, len(neighbours))
                passed = True
            level_copy(0, c).start()
            if c == 0:
                tell(0)
        elif event[0] == "s":
            _, k, c = event
            if event == ("s", 1, 0):
                small[1].wait()
            if event in ROUNDS:
                hear(ROUNDS.index(event))
                if event != ROUNDS[-1]:
                    tell(ROUNDS.index(event) + 1)
            if k == 1:
                all_loads[c][2].wait()
                own_terms(0, c)
            level_event(k - 1, c)
            if k < LEVELS:
                level_copy(k, c).start()
                own_terms(k, c)
        elif event[0] == "a":
            a2a_event(event[1])
        elif event[0] == "p":
            root_copy.start()
            prepare_perm()
            prepare_pick()
        else:
            root_event(event[1])
    for k in range(LEVELS):
        for c in range(CHUNKS):
            level_copy(k, c).wait_send()
    for g in range(len(GROUPS)):
        a2a_bytes(g, N_ORDER - 1).wait_send()
    for copy in (pick_copy, part_copy, coef_copy):
        copy.wait()


def finish_kernel(part_hbm, coef_hbm, pick_hbm, out_hbm, part, coef_t, pick, out, in_sem, out_sem):
    copies = [
        pltpu.make_async_copy(coef_hbm, coef_t, in_sem.at[0]),
        pltpu.make_async_copy(pick_hbm, pick, in_sem.at[1]),
        pltpu.make_async_copy(part_hbm, part, in_sem.at[2]),
    ]
    for copy in copies:
        copy.start()
    degree = lax.axis_index("lat") * 128 + lax.broadcasted_iota(I32, (128, 512), 0)
    window = DEGREES // 512 * lax.broadcasted_iota(I32, (128, 512), 1)
    alive = degree >= window
    for copy in copies:
        copy.wait()
    natural = jnp.dot(coef_t[...].reshape(512, 128), pick[...], preferred_element_type=F32)
    out_copies = []
    for cc in range(4):
        rows = slice(cc * 128, (cc + 1) * 128)
        total = part[rows].astype(F32) + natural[rows]
        out[cc] = jnp.where(alive, total, 0.0).astype(BF16)
        copy = pltpu.make_async_copy(out.at[cc], out_hbm.at[cc // 2, cc % 2], out_sem.at[cc])
        copy.start()
        out_copies.append(copy)
    for copy in out_copies:
        copy.wait()


def per_device(
    fourier, quad_weights, leaf_basis, level_factors, sparsity, root_basis, order_of_slot
):
    anywhere = pl.BlockSpec(memory_space=pl.ANY)
    vmem = pltpu.VMEM
    parts = pl.pallas_call(
        kernel,
        out_shape=[
            jax.ShapeDtypeStruct((512, 512), BF16),
            jax.ShapeDtypeStruct((4, 128, 128), BF16),
            jax.ShapeDtypeStruct((128, 512), BF16),
        ],
        in_specs=[anywhere] * 7,
        out_specs=[anywhere] * 3,
        scratch_shapes=[
            vmem((SLOTS, 64, 128), BF16),
            vmem((1, 128), F32),
            vmem((SLOTS, 64, 128), BF16),
            vmem((SLOTS, LEVELS, 2, 64, 64), BF16),
            pltpu.SMEM((LEVELS, 1, SLOTS), I32),
            vmem((512, 64, 128), BF16),
            vmem((4, 128), I32),
            vmem((LEVELS + 1, CHUNKS, 2, RANK, 128), BF16),
            vmem((LEVELS, CHUNKS, 2, RANK, 128), BF16),
            vmem((LEVELS, CHUNKS, 2, RANK, 128), F32),
            vmem((256, 256), BF16),
            vmem((len(GROUPS), N_ORDER, 16, 128), BF16),
            vmem((len(GROUPS), N_ORDER, 16, 128), BF16),
            vmem((512, 128), F32),
            vmem((512, 512), BF16),
            vmem((512, 128), F32),
            vmem((4, 128, 512), BF16),
            vmem((512, 512), BF16),
            pltpu.SemaphoreType.DMA((3, CHUNKS)),
            pltpu.SemaphoreType.DMA((3,)),
            pltpu.SemaphoreType.DMA,
            pltpu.SemaphoreType.DMA((3,)),
            pltpu.SemaphoreType.DMA((LEVELS, CHUNKS)),
            pltpu.SemaphoreType.DMA((LEVELS, CHUNKS)),
            pltpu.SemaphoreType.DMA((len(GROUPS),)),
            pltpu.SemaphoreType.DMA((len(GROUPS), 2)),
            pltpu.SemaphoreType.REGULAR((3,)),
        ],
        compiler_params=pltpu.CompilerParams(
            collective_id=0, has_side_effects=True, vmem_limit_bytes=60 * 1024 * 1024
        ),
        cost_estimate=pl.CostEstimate(
            flops=2 * 10**9, bytes_accessed=15 * 10**6, transcendentals=0
        ),
    )(
        fourier,
        quad_weights.reshape(1, 128),
        leaf_basis,
        level_factors,
        sparsity.transpose(1, 2, 0),
        root_basis,
        order_of_slot.reshape(4, 128),
    )
    return pl.pallas_call(
        finish_kernel,
        out_shape=jax.ShapeDtypeStruct((2, 2, 128, 512), BF16),
        in_specs=[anywhere] * 3,
        out_specs=anywhere,
        scratch_shapes=[
            vmem((512, 512), BF16),
            vmem((4, 128, 128), BF16),
            vmem((128, 512), BF16),
            vmem((4, 128, 512), BF16),
            pltpu.SemaphoreType.DMA((3,)),
            pltpu.SemaphoreType.DMA((4,)),
        ],
        compiler_params=pltpu.CompilerParams(vmem_limit_bytes=60 * 1024 * 1024),
        cost_estimate=pl.CostEstimate(
            flops=2**26, bytes_accessed=5 * 2**18, transcendentals=0
        ),
    )(*parts)


def solution(mesh):
    return jax.shard_map(
        per_device,
        mesh=mesh,
        in_specs=(
            P("order", None, "lat"),
            P("lat"),
            P("order", None, "lat"),
            P("order", None, None, "lat", None, None),
            P("order", None, "lat"),
            P(None, None, "lat"),
            P(),
        ),
        out_specs=P("order", None, "lat", None),
        check_vma=False,
    )
```

```python
import functools

import jax
import jax.numpy as jnp
from jax import lax
from jax.experimental import pallas as pl
from jax.experimental.pallas import tpu as pltpu
from jax.sharding import PartitionSpec as P

DEGREES = 2048
MESH = pl.DeviceIdType.MESH
BF16 = jnp.bfloat16
F32 = jnp.float32
I32 = jnp.int32

SLOTS = 32
CHUNK = 4
CHUNKS = SLOTS // CHUNK
LEVELS = 4
GROUPS = ((0, 1), (2, 3), (4, 5), (6,), (7,))
LAST = len(GROUPS) - 1
N_ORDER = 16
RANK = 64


HOPS = [(0, 1, 2, 1)[k >> 2] + (0, 1, 2, 1)[k & 3] for k in range(N_ORDER)]
NEAR = [k for k in range(1, N_ORDER) if HOPS[k] <= 2]
FAR = [k for k in range(1, N_ORDER) if HOPS[k] > 2]


def schedule():
    keyed = []
    for c in range(CHUNKS):
        keyed.append((c * 1.0, 0, ("s", 0, c)))
        keyed.append((c * 1.0 + 2.5, 1, ("s", 1, c)))
        keyed.append((c * 1.0 + 5.5, 2, ("s", 2, c)))
        keyed.append((c * 2.0 + 12.0, 3, ("s", 3, c)))
        keyed.append((c * 2.0 + 18.5, 4, ("s", 4, c)))
    for g, chunks in enumerate(GROUPS):
        keyed.append((chunks[-1] * 2.0 + 18.6, 5, ("a", g)))
        keyed.append((999 + g, 6, ("r", g)))
    keyed.append((8.1, 7, ("p",)))
    return [event for _, _, event in sorted(keyed)]


ROUNDS = [("s", 2, c) for c in range(3, 8)]


def kernel(
    four_hbm, quad_hbm, leaf_hbm, fac_hbm, spars_hbm, root_hbm, order_hbm, part_hbm, coef_hbm, pick_hbm,
    four, quad, leaf, fac, spars, root, order,
    state, partner, own, perm, send_buf, recv_buf, order_col, pick, coef, coef_t, part,
    in_sem, small_sem, root_sem, out_sem, send_sem, recv_sem, a2a_send_sem, a2a_recv_sem, near_sem, column_sem, order_sem, round_sem, told_sem,
):
    me_o = lax.axis_index("order")
    me_l = lax.axis_index("lat")
    peers = [me_l ^ (1 << k) for k in range(LEVELS)]

    def loads(c):
        span = pl.ds(c * CHUNK, CHUNK)
        return [
            pltpu.make_async_copy(four_hbm.at[span], four.at[span], in_sem.at[0, c]),
            pltpu.make_async_copy(leaf_hbm.at[span], leaf.at[span], in_sem.at[1, c]),
            pltpu.make_async_copy(fac_hbm.at[span, :, :, 0], fac.at[span], in_sem.at[2, c]),
        ]

    small = [
        pltpu.make_async_copy(quad_hbm, quad, small_sem.at[0]),
        pltpu.make_async_copy(spars_hbm, spars, small_sem.at[1]),
        pltpu.make_async_copy(order_hbm, order, small_sem.at[2]),
    ]
    root_copy = pltpu.make_async_copy(root_hbm, root, root_sem)
    all_loads = [loads(c) for c in range(CHUNKS)]
    for copy in (all_loads[0][0], all_loads[0][1], small[0]):
        copy.start()

    z, core = me_l // 2, lax.rem(me_l, 2)
    bottom = z == 0
    low_bit = [lax.rem(me_l // (1 << k), 2) == 0 for k in range(LEVELS)]
    order_low = [lax.rem(me_o // (1 << i), 2) == 0 for i in range(4)]
    order_peers = [(me_o ^ (1 << i), me_l) for i in range(4)]
    far_z = (3, 5, 6, 7)

    def signal(sem, place):
        pl.semaphore_signal(sem, inc=1, device_id=place, device_id_type=MESH)

    def upper(flag):
        return jnp.logical_not(flag).astype(I32)

    barrier = pltpu.get_barrier_semaphore()
    signal(barrier, (me_o, peers[0]))
    for k in range(1, LEVELS):

        @pl.when(low_bit[k])
        def _():
            signal(barrier, (me_o, peers[k]))

    @pl.when(bottom)
    def _():
        for far in far_z:
            signal(barrier, (me_o, far * 2 + core))
        for i in range(4):

            @pl.when(order_low[i])
            def _():
                signal(barrier, order_peers[i])

    bits = sum(upper(low_bit[k]) for k in range(1, LEVELS))
    order_bits = sum(upper(order_low[i]) for i in range(4))
    expected = (
        1 + bits + (bits >= 2).astype(I32) + jnp.where(bottom, order_bits, jnp.zeros_like(order_bits))
    )

    def enter():
        pl.semaphore_wait(barrier, expected)

    def answer():
        for k in range(1, LEVELS):

            @pl.when(jnp.logical_not(low_bit[k]))
            def _():
                signal(near_sem.at[k], (me_o, peers[k]))

        @pl.when(jnp.logical_not(bottom))
        def _():
            signal(column_sem, (me_o, core))

        @pl.when(bottom)
        def _():
            for i in range(4):

                @pl.when(jnp.logical_not(order_low[i]))
                def _():
                    signal(order_sem.at[i], order_peers[i])

    def hear(k):
        @pl.when(low_bit[k])
        def _():
            pl.semaphore_wait(near_sem.at[k], 1)

    def order_round(n):
        @pl.when(bottom)
        def _():
            if n == 0:
                pl.semaphore_wait(column_sem, 7)
                for i in range(4):

                    @pl.when(order_low[i])
                    def _():
                        pl.semaphore_wait(order_sem.at[i], 1)

            else:
                pl.semaphore_wait(round_sem.at[n - 1], 1)
            if n < 4:
                signal(round_sem.at[n], order_peers[n])
            else:
                for up in range(1, 8):
                    signal(told_sem, (me_o, up * 2 + core))

    def told():
        @pl.when(jnp.logical_not(bottom))
        def _():
            pl.semaphore_wait(told_sem, 1)

    for c in range(1, CHUNKS):
        for copy in all_loads[c][:2]:
            copy.start()
    for copy in small[1:]:
        copy.start()
    for c in range(CHUNKS):
        all_loads[c][2].start()

    def level_copy(k, c):
        return pltpu.make_async_remote_copy(
            src_ref=state.at[k, c],
            dst_ref=partner.at[k, c],
            send_sem=send_sem.at[k, c],
            recv_sem=recv_sem.at[k, c],
            device_id=(me_o, peers[k]),
            device_id_type=MESH,
        )

    def a2a_copy(g, k):
        return pltpu.make_async_remote_copy(
            src_ref=send_buf.at[g, me_o ^ k],
            dst_ref=recv_buf.at[g, k],
            send_sem=a2a_send_sem.at[g],
            recv_sem=a2a_recv_sem.at[g, int(g == LAST and k in FAR)],
            device_id=(me_o ^ k, me_l),
            device_id_type=MESH,
        )

    def a2a_bytes(g, count, far=0):
        return pltpu.make_async_remote_copy(
            src_ref=send_buf.at[g, pl.ds(0, count)],
            dst_ref=recv_buf.at[g, pl.ds(0, count)],
            send_sem=a2a_send_sem.at[g],
            recv_sem=a2a_recv_sem.at[g, far],
            device_id=(me_o ^ 1, me_l),
            device_id_type=MESH,
        )

    low = lax.broadcasted_iota(I32, (RANK, 128), 1) < RANK

    def both(a, b):
        return jnp.concatenate([a, b], axis=0)

    def diagonal(product):
        return jnp.where(low, product[:RANK], product[RANK:])

    def own_terms(k, c):
        for h in range(2):
            s0, s1 = c * CHUNK + h, c * CHUNK + 2 + h
            a = both(fac[s0, k, 0], fac[s1, k, 0])
            own[k, c, h] = diagonal(jnp.dot(a, state[k, c, h], preferred_element_type=F32))

    def start_event(c):
        for copy in all_loads[c][:2]:
            copy.wait()
        w = quad[...]
        for h in range(2):
            s0, s1 = c * CHUNK + h, c * CHUNK + 2 + h
            weighted = both(
                (four[s0].astype(F32) * w).astype(BF16), (four[s1].astype(F32) * w).astype(BF16)
            )
            basis = both(leaf[s0], leaf[s1])
            product = lax.dot_general(
                basis, weighted, (((1,), (1,)), ((), ())), preferred_element_type=F32
            )
            state[0, c, h] = diagonal(product).astype(BF16)

    def level_event(k, c):
        level_copy(k, c).wait_recv()
        for h in range(2):
            s0, s1 = c * CHUNK + h, c * CHUNK + 2 + h
            b = both(fac[s0, k, 1], fac[s1, k, 1])
            cross = diagonal(jnp.dot(b, partner[k, c, h], preferred_element_type=F32))
            present = jnp.where(low, spars[k, 0, s0], spars[k, 0, s1]).astype(F32)
            state[k + 1, c, h] = (own[k, c, h] + present * cross).astype(BF16)

    def a2a_event(g):
        x = [state[LEVELS, c].reshape(2 * RANK, 128) for c in GROUPS[g]]
        packed = lax.dot_general(
            perm[:, : 128 * len(x)],
            jnp.concatenate(x, axis=1),
            (((1,), (1,)), ((), ())),
            preferred_element_type=F32,
        ).astype(BF16)
        send_buf[g] = packed.reshape(N_ORDER, 16, 128)
        for k in sorted(NEAR + FAR, key=lambda k: -HOPS[k]):
            a2a_copy(g, k).start()
        recv_buf[g, 0] = send_buf[g, me_o]

    def prepare_perm():
        row = lax.broadcasted_iota(I32, (256, 256), 0)
        col = lax.broadcasted_iota(I32, (256, 256), 1)
        target = (row & 3) * 64 + (row >> 4) * 4 + ((row >> 2) & 3)
        perm[...] = (col == target).astype(F32).astype(BF16)

    def prepare_pick():
        small[2].wait()
        orders = order[...].astype(F32)
        for i in range(4):
            wide = jnp.broadcast_to(orders[i : i + 1], (128, 128))
            order_col[pl.ds(i * 128, 128)] = wide.T
        window = lax.broadcasted_iota(I32, (16, 512), 1).astype(F32)
        for g in range(SLOTS // 8):
            for q in range(4):
                for h in range(2):
                    col = order_col[pl.ds(8 * g + 2 * q + h, 16, stride=SLOTS), :]
                    wide = jnp.concatenate([col] * 4, axis=1)
                    row = g * 128 + q * 32 + h * 16
                    pick[pl.ds(row, 16)] = (wide == window).astype(F32).astype(BF16)
        pick_copy.start()

    def root_event(g):
        if g == 0:
            root_copy.wait()
        pair = len(GROUPS[g]) == 2
        row = lax.broadcasted_iota(I32, (32, 256), 0)
        col = lax.broadcasted_iota(I32, (32, 256), 1)
        keep = ((row >> 4) == ((col >> 6) & 1)) & ((row & 1) == (col >> 7))
        keep = keep.astype(F32).astype(BF16)
        first = (lax.broadcasted_iota(I32, (32, 128), 0) & 2) == 0

        def one(k):
            source = me_o ^ k
            r = recv_buf[g, k]
            r2 = jnp.concatenate([r, r], axis=1)
            lhs = jnp.concatenate([r2, r2], axis=0) * keep
            base = source * SLOTS + GROUPS[g][0] * CHUNK
            w = root[pl.ds(base, 4)].reshape(256, 128)
            if pair:
                w = jnp.concatenate([w, root[pl.ds(base + 4, 4)].reshape(256, 128)], axis=1)
            product = jnp.dot(lhs, w, preferred_element_type=F32)
            if pair:
                product = jnp.where(first, product[:, :128], product[:, 128:])
            coef[pl.ds(pl.multiple_of(source * 32, 32), 32)] = product

        if g == LAST:
            one(0)
            a2a_bytes(g, len(NEAR), 0).wait_recv()
            for k in NEAR:
                one(k)
            a2a_bytes(g, len(FAR), 1).wait_recv()
            for k in FAR:
                one(k)
        else:
            a2a_bytes(g, N_ORDER - 1).wait_recv()

            def body(k, carry):
                one(k)
                return carry

            lax.fori_loop(0, N_ORDER, body, 0, unroll=4)
        width = 128 if pair else 64
        lanes = pl.ds(GROUPS[g][0] * 64, width)
        for cc in range(4):
            parts = []
            for q in range(width // 32):
                for h in range(2):
                    parts.append(coef[pl.ds(h * 16 + cc * 4 + q, 16, stride=32), :])
            coef_t[cc, :, lanes] = jnp.concatenate(parts, axis=0).T.astype(BF16)
        if g == 2:
            part[...] = jnp.dot(
                coef_t[:, :, :384].reshape(512, 384), pick[:384], preferred_element_type=F32
            ).astype(BF16)
            part_copy.start()
        if g == LAST:
            coef_copy.start()

    coef_copy = pltpu.make_async_copy(coef_t.at[:, :, pl.ds(384, 128)], coef_hbm, out_sem.at[0])
    pick_copy = pltpu.make_async_copy(pick.at[pl.ds(384, 128)], pick_hbm, out_sem.at[1])
    part_copy = pltpu.make_async_copy(part, part_hbm, out_sem.at[2])

    small[0].wait()
    passed = False
    for event in schedule():
        if event[0] == "s" and event[1] == 0:
            c = event[2]
            start_event(c)
            if not passed:
                enter()
                passed = True
            level_copy(0, c).start()
            if c == 0:
                answer()
        elif event[0] == "s":
            _, k, c = event
            if event == ("s", 1, 0):
                small[1].wait()
            if event in ROUNDS:
                order_round(ROUNDS.index(event))
            if k == 1:
                all_loads[c][2].wait()
                own_terms(0, c)
            level_event(k - 1, c)
            if c == 0 and k < LEVELS:
                hear(k)
            if k < LEVELS:
                level_copy(k, c).start()
                own_terms(k, c)
        elif event[0] == "a":
            if event[1] == 0:
                told()
            a2a_event(event[1])
        elif event[0] == "p":
            root_copy.start()
            prepare_perm()
            prepare_pick()
        else:
            root_event(event[1])
    for k in range(LEVELS):
        for c in range(CHUNKS):
            level_copy(k, c).wait_send()
    for g in range(len(GROUPS)):
        a2a_bytes(g, N_ORDER - 1).wait_send()
    for copy in (pick_copy, part_copy, coef_copy):
        copy.wait()


def finish_kernel(part_hbm, coef_hbm, pick_hbm, out_hbm, part, coef_t, pick, out, in_sem, out_sem):
    copies = [
        pltpu.make_async_copy(coef_hbm, coef_t, in_sem.at[0]),
        pltpu.make_async_copy(pick_hbm, pick, in_sem.at[1]),
        pltpu.make_async_copy(part_hbm, part, in_sem.at[2]),
    ]
    for copy in copies:
        copy.start()
    degree = lax.axis_index("lat") * 128 + lax.broadcasted_iota(I32, (128, 512), 0)
    window = DEGREES // 512 * lax.broadcasted_iota(I32, (128, 512), 1)
    alive = degree >= window
    for copy in copies:
        copy.wait()
    natural = jnp.dot(coef_t[...].reshape(512, 128), pick[...], preferred_element_type=F32)
    out_copies = []
    for cc in range(4):
        rows = slice(cc * 128, (cc + 1) * 128)
        total = part[rows].astype(F32) + natural[rows]
        out[cc] = jnp.where(alive, total, 0.0).astype(BF16)
        copy = pltpu.make_async_copy(out.at[cc], out_hbm.at[cc // 2, cc % 2], out_sem.at[cc])
        copy.start()
        out_copies.append(copy)
    for copy in out_copies:
        copy.wait()


def per_device(
    fourier, quad_weights, leaf_basis, level_factors, sparsity, root_basis, order_of_slot
):
    anywhere = pl.BlockSpec(memory_space=pl.ANY)
    vmem = pltpu.VMEM
    parts = pl.pallas_call(
        kernel,
        out_shape=[
            jax.ShapeDtypeStruct((512, 512), BF16),
            jax.ShapeDtypeStruct((4, 128, 128), BF16),
            jax.ShapeDtypeStruct((128, 512), BF16),
        ],
        in_specs=[anywhere] * 7,
        out_specs=[anywhere] * 3,
        scratch_shapes=[
            vmem((SLOTS, 64, 128), BF16),
            vmem((1, 128), F32),
            vmem((SLOTS, 64, 128), BF16),
            vmem((SLOTS, LEVELS, 2, 64, 64), BF16),
            pltpu.SMEM((LEVELS, 1, SLOTS), I32),
            vmem((512, 64, 128), BF16),
            vmem((4, 128), I32),
            vmem((LEVELS + 1, CHUNKS, 2, RANK, 128), BF16),
            vmem((LEVELS, CHUNKS, 2, RANK, 128), BF16),
            vmem((LEVELS, CHUNKS, 2, RANK, 128), F32),
            vmem((256, 256), BF16),
            vmem((len(GROUPS), N_ORDER, 16, 128), BF16),
            vmem((len(GROUPS), N_ORDER, 16, 128), BF16),
            vmem((512, 128), F32),
            vmem((512, 512), BF16),
            vmem((512, 128), F32),
            vmem((4, 128, 512), BF16),
            vmem((512, 512), BF16),
            pltpu.SemaphoreType.DMA((3, CHUNKS)),
            pltpu.SemaphoreType.DMA((3,)),
            pltpu.SemaphoreType.DMA,
            pltpu.SemaphoreType.DMA((3,)),
            pltpu.SemaphoreType.DMA((LEVELS, CHUNKS)),
            pltpu.SemaphoreType.DMA((LEVELS, CHUNKS)),
            pltpu.SemaphoreType.DMA((len(GROUPS),)),
            pltpu.SemaphoreType.DMA((len(GROUPS), 2)),
            pltpu.SemaphoreType.REGULAR((LEVELS,)),
            pltpu.SemaphoreType.REGULAR,
            pltpu.SemaphoreType.REGULAR((4,)),
            pltpu.SemaphoreType.REGULAR((4,)),
            pltpu.SemaphoreType.REGULAR,
        ],
        compiler_params=pltpu.CompilerParams(
            collective_id=0, has_side_effects=True, vmem_limit_bytes=60 * 1024 * 1024
        ),
        cost_estimate=pl.CostEstimate(
            flops=2 * 10**9, bytes_accessed=15 * 10**6, transcendentals=0
        ),
    )(
        fourier,
        quad_weights.reshape(1, 128),
        leaf_basis,
        level_factors,
        sparsity.transpose(1, 2, 0),
        root_basis,
        order_of_slot.reshape(4, 128),
    )
    return pl.pallas_call(
        finish_kernel,
        out_shape=jax.ShapeDtypeStruct((2, 2, 128, 512), BF16),
        in_specs=[anywhere] * 3,
        out_specs=anywhere,
        scratch_shapes=[
            vmem((512, 512), BF16),
            vmem((4, 128, 128), BF16),
            vmem((128, 512), BF16),
            vmem((4, 128, 512), BF16),
            pltpu.SemaphoreType.DMA((3,)),
            pltpu.SemaphoreType.DMA((4,)),
        ],
        compiler_params=pltpu.CompilerParams(vmem_limit_bytes=60 * 1024 * 1024),
        cost_estimate=pl.CostEstimate(
            flops=2**26, bytes_accessed=5 * 2**18, transcendentals=0
        ),
    )(*parts)


def solution(mesh):
    return jax.shard_map(
        per_device,
        mesh=mesh,
        in_specs=(
            P("order", None, "lat"),
            P("lat"),
            P("order", None, "lat"),
            P("order", None, None, "lat", None, None),
            P("order", None, "lat"),
            P(None, None, "lat"),
            P(),
        ),
        out_specs=P("order", None, "lat", None),
        check_vma=False,
    )
```

```python
import functools

import jax
import jax.numpy as jnp
from jax import lax
from jax.experimental import pallas as pl
from jax.experimental.pallas import tpu as pltpu
from jax.sharding import PartitionSpec as P

DEGREES = 2048
MESH = pl.DeviceIdType.MESH
BF16 = jnp.bfloat16
F32 = jnp.float32
I32 = jnp.int32

SLOTS = 32
CHUNK = 4
CHUNKS = SLOTS // CHUNK
LEVELS = 4
GROUPS = ((0, 1), (2, 3), (4, 5), (6,), (7,))
LAST = len(GROUPS) - 1
N_ORDER = 16
RANK = 64
HUB = 6


HOPS = [(0, 1, 2, 1)[k >> 2] + (0, 1, 2, 1)[k & 3] for k in range(N_ORDER)]
NEAR = [k for k in range(1, N_ORDER) if HOPS[k] <= 2]
FAR = [k for k in range(1, N_ORDER) if HOPS[k] > 2]


def schedule():
    keyed = []
    for c in range(CHUNKS):
        keyed.append((c * 1.0, 0, ("s", 0, c)))
        keyed.append((c * 1.0 + 2.5, 1, ("s", 1, c)))
        keyed.append((c * 1.0 + 5.5, 2, ("s", 2, c)))
        keyed.append((c * 2.0 + 12.0, 3, ("s", 3, c)))
        keyed.append((c * 2.0 + 18.5, 4, ("s", 4, c)))
    for g, chunks in enumerate(GROUPS):
        keyed.append((chunks[-1] * 2.0 + 18.6, 5, ("a", g)))
        keyed.append((999 + g, 6, ("r", g)))
    keyed.append((8.1, 7, ("p",)))
    return [event for _, _, event in sorted(keyed)]


ROUNDS = [("s", 2, c) for c in range(3, 8)]


def kernel(
    four_hbm, quad_hbm, leaf_hbm, fac_hbm, spars_hbm, root_hbm, order_hbm, part_hbm, coef_hbm, pick_hbm,
    four, quad, leaf, fac, spars, root, order,
    state, partner, own, perm, send_buf, recv_buf, order_col, pick, coef, coef_t, part,
    in_sem, small_sem, root_sem, out_sem, send_sem, recv_sem, a2a_send_sem, a2a_recv_sem, near_sem, order_sem, round_sem, told_sem,
):
    me_o = lax.axis_index("order")
    me_l = lax.axis_index("lat")
    peers = [me_l ^ (1 << k) for k in range(LEVELS)]

    def loads(c):
        span = pl.ds(c * CHUNK, CHUNK)
        return [
            pltpu.make_async_copy(four_hbm.at[span], four.at[span], in_sem.at[0, c]),
            pltpu.make_async_copy(leaf_hbm.at[span], leaf.at[span], in_sem.at[1, c]),
            pltpu.make_async_copy(fac_hbm.at[span, :, :, 0], fac.at[span], in_sem.at[2, c]),
        ]

    small = [
        pltpu.make_async_copy(quad_hbm, quad, small_sem.at[0]),
        pltpu.make_async_copy(spars_hbm, spars, small_sem.at[1]),
        pltpu.make_async_copy(order_hbm, order, small_sem.at[2]),
    ]
    root_copy = pltpu.make_async_copy(root_hbm, root, root_sem)
    all_loads = [loads(c) for c in range(CHUNKS)]
    for copy in (all_loads[0][0], all_loads[0][1], small[0]):
        copy.start()

    z, core = me_l // 2, lax.rem(me_l, 2)
    hub = z == HUB
    low_bit = [lax.rem(me_l // (1 << k), 2) == 0 for k in range(LEVELS)]
    order_low = [lax.rem(me_o // (1 << i), 2) == 0 for i in range(4)]
    order_peers = [(me_o ^ (1 << i), me_l) for i in range(4)]
    far_z = [low for low in range(HUB) if HUB ^ low not in (1, 2, 4)]

    def signal(sem, place):
        pl.semaphore_signal(sem, inc=1, device_id=place, device_id_type=MESH)

    def upper(flag):
        return jnp.logical_not(flag).astype(I32)

    barrier = pltpu.get_barrier_semaphore()
    signal(barrier, (me_o, peers[0]))
    for k in range(1, LEVELS):

        @pl.when(low_bit[k])
        def _():
            signal(barrier, (me_o, peers[k]))

    for low in far_z:

        @pl.when(z == low)
        def _():
            signal(barrier, (me_o, HUB * 2 + core))

    @pl.when(hub)
    def _():
        for i in range(4):

            @pl.when(order_low[i])
            def _():
                signal(barrier, order_peers[i])

    bits = sum(upper(low_bit[k]) for k in range(1, LEVELS))
    order_bits = sum(upper(order_low[i]) for i in range(4))
    expected = 1 + bits + hub.astype(I32) * (order_bits + len(far_z))

    def enter():
        pl.semaphore_wait(barrier, expected)

    def answer():
        for k in range(1, LEVELS):

            @pl.when(jnp.logical_not(low_bit[k]))
            def _():
                signal(near_sem.at[k], (me_o, peers[k]))

        @pl.when(hub)
        def _():
            for i in range(4):

                @pl.when(jnp.logical_not(order_low[i]))
                def _():
                    signal(order_sem.at[i], order_peers[i])

    def hear(k):
        @pl.when(low_bit[k])
        def _():
            pl.semaphore_wait(near_sem.at[k], 1)

    def order_round(n):
        @pl.when(hub)
        def _():
            if n == 0:
                for i in range(4):

                    @pl.when(order_low[i])
                    def _():
                        pl.semaphore_wait(order_sem.at[i], 1)

            else:
                pl.semaphore_wait(round_sem.at[n - 1], 1)
            if n < 4:
                signal(round_sem.at[n], order_peers[n])
            else:
                for other in range(8):
                    if other != HUB:
                        signal(told_sem, (me_o, other * 2 + core))

    def told():
        @pl.when(jnp.logical_not(hub))
        def _():
            pl.semaphore_wait(told_sem, 1)

    for c in range(1, CHUNKS):
        for copy in all_loads[c][:2]:
            copy.start()
    for copy in small[1:]:
        copy.start()
    for c in range(CHUNKS):
        all_loads[c][2].start()

    def level_copy(k, c):
        return pltpu.make_async_remote_copy(
            src_ref=state.at[k, c],
            dst_ref=partner.at[k, c],
            send_sem=send_sem.at[k, c],
            recv_sem=recv_sem.at[k, c],
            device_id=(me_o, peers[k]),
            device_id_type=MESH,
        )

    def a2a_copy(g, k):
        return pltpu.make_async_remote_copy(
            src_ref=send_buf.at[g, me_o ^ k],
            dst_ref=recv_buf.at[g, k],
            send_sem=a2a_send_sem.at[g],
            recv_sem=a2a_recv_sem.at[g, int(g == LAST and k in FAR)],
            device_id=(me_o ^ k, me_l),
            device_id_type=MESH,
        )

    def a2a_bytes(g, count, far=0):
        return pltpu.make_async_remote_copy(
            src_ref=send_buf.at[g, pl.ds(0, count)],
            dst_ref=recv_buf.at[g, pl.ds(0, count)],
            send_sem=a2a_send_sem.at[g],
            recv_sem=a2a_recv_sem.at[g, far],
            device_id=(me_o ^ 1, me_l),
            device_id_type=MESH,
        )

    low = lax.broadcasted_iota(I32, (RANK, 128), 1) < RANK

    def both(a, b):
        return jnp.concatenate([a, b], axis=0)

    def diagonal(product):
        return jnp.where(low, product[:RANK], product[RANK:])

    def own_terms(k, c):
        for h in range(2):
            s0, s1 = c * CHUNK + h, c * CHUNK + 2 + h
            a = both(fac[s0, k, 0], fac[s1, k, 0])
            own[k, c, h] = diagonal(jnp.dot(a, state[k, c, h], preferred_element_type=F32))

    def start_event(c):
        for copy in all_loads[c][:2]:
            copy.wait()
        w = quad[...]
        for h in range(2):
            s0, s1 = c * CHUNK + h, c * CHUNK + 2 + h
            weighted = both(
                (four[s0].astype(F32) * w).astype(BF16), (four[s1].astype(F32) * w).astype(BF16)
            )
            basis = both(leaf[s0], leaf[s1])
            product = lax.dot_general(
                basis, weighted, (((1,), (1,)), ((), ())), preferred_element_type=F32
            )
            state[0, c, h] = diagonal(product).astype(BF16)

    def level_event(k, c):
        level_copy(k, c).wait_recv()
        for h in range(2):
            s0, s1 = c * CHUNK + h, c * CHUNK + 2 + h
            b = both(fac[s0, k, 1], fac[s1, k, 1])
            cross = diagonal(jnp.dot(b, partner[k, c, h], preferred_element_type=F32))
            present = jnp.where(low, spars[k, 0, s0], spars[k, 0, s1]).astype(F32)
            state[k + 1, c, h] = (own[k, c, h] + present * cross).astype(BF16)

    def a2a_event(g):
        x = [state[LEVELS, c].reshape(2 * RANK, 128) for c in GROUPS[g]]
        packed = lax.dot_general(
            perm[:, : 128 * len(x)],
            jnp.concatenate(x, axis=1),
            (((1,), (1,)), ((), ())),
            preferred_element_type=F32,
        ).astype(BF16)
        send_buf[g] = packed.reshape(N_ORDER, 16, 128)
        for k in sorted(NEAR + FAR, key=lambda k: -HOPS[k]):
            a2a_copy(g, k).start()
        recv_buf[g, 0] = send_buf[g, me_o]

    def prepare_perm():
        row = lax.broadcasted_iota(I32, (256, 256), 0)
        col = lax.broadcasted_iota(I32, (256, 256), 1)
        target = (row & 3) * 64 + (row >> 4) * 4 + ((row >> 2) & 3)
        perm[...] = (col == target).astype(F32).astype(BF16)

    def prepare_pick():
        small[2].wait()
        orders = order[...].astype(F32)
        for i in range(4):
            wide = jnp.broadcast_to(orders[i : i + 1], (128, 128))
            order_col[pl.ds(i * 128, 128)] = wide.T
        window = lax.broadcasted_iota(I32, (16, 512), 1).astype(F32)
        for g in range(SLOTS // 8):
            for q in range(4):
                for h in range(2):
                    col = order_col[pl.ds(8 * g + 2 * q + h, 16, stride=SLOTS), :]
                    wide = jnp.concatenate([col] * 4, axis=1)
                    row = g * 128 + q * 32 + h * 16
                    pick[pl.ds(row, 16)] = (wide == window).astype(F32).astype(BF16)
        pick_copy.start()

    def root_event(g):
        if g == 0:
            root_copy.wait()
        pair = len(GROUPS[g]) == 2
        row = lax.broadcasted_iota(I32, (32, 256), 0)
        col = lax.broadcasted_iota(I32, (32, 256), 1)
        keep = ((row >> 4) == ((col >> 6) & 1)) & ((row & 1) == (col >> 7))
        keep = keep.astype(F32).astype(BF16)
        first = (lax.broadcasted_iota(I32, (32, 128), 0) & 2) == 0

        def one(k):
            source = me_o ^ k
            r = recv_buf[g, k]
            r2 = jnp.concatenate([r, r], axis=1)
            lhs = jnp.concatenate([r2, r2], axis=0) * keep
            base = source * SLOTS + GROUPS[g][0] * CHUNK
            w = root[pl.ds(base, 4)].reshape(256, 128)
            if pair:
                w = jnp.concatenate([w, root[pl.ds(base + 4, 4)].reshape(256, 128)], axis=1)
            product = jnp.dot(lhs, w, preferred_element_type=F32)
            if pair:
                product = jnp.where(first, product[:, :128], product[:, 128:])
            coef[pl.ds(pl.multiple_of(source * 32, 32), 32)] = product

        if g == LAST:
            one(0)
            a2a_bytes(g, len(NEAR), 0).wait_recv()
            for k in NEAR:
                one(k)
            a2a_bytes(g, len(FAR), 1).wait_recv()
            for k in FAR:
                one(k)
        else:
            a2a_bytes(g, N_ORDER - 1).wait_recv()

            def body(k, carry):
                one(k)
                return carry

            lax.fori_loop(0, N_ORDER, body, 0, unroll=4)
        width = 128 if pair else 64
        lanes = pl.ds(GROUPS[g][0] * 64, width)
        for cc in range(4):
            parts = []
            for q in range(width // 32):
                for h in range(2):
                    parts.append(coef[pl.ds(h * 16 + cc * 4 + q, 16, stride=32), :])
            coef_t[cc, :, lanes] = jnp.concatenate(parts, axis=0).T.astype(BF16)
        if g == 2:
            part[...] = jnp.dot(
                coef_t[:, :, :384].reshape(512, 384), pick[:384], preferred_element_type=F32
            ).astype(BF16)
            part_copy.start()
        if g == LAST:
            coef_copy.start()

    coef_copy = pltpu.make_async_copy(coef_t.at[:, :, pl.ds(384, 128)], coef_hbm, out_sem.at[0])
    pick_copy = pltpu.make_async_copy(pick.at[pl.ds(384, 128)], pick_hbm, out_sem.at[1])
    part_copy = pltpu.make_async_copy(part, part_hbm, out_sem.at[2])

    small[0].wait()
    passed = False
    for event in schedule():
        if event[0] == "s" and event[1] == 0:
            c = event[2]
            start_event(c)
            if not passed:
                enter()
                passed = True
            level_copy(0, c).start()
            if c == 0:
                answer()
        elif event[0] == "s":
            _, k, c = event
            if event == ("s", 1, 0):
                small[1].wait()
            if event in ROUNDS:
                order_round(ROUNDS.index(event))
            if k == 1:
                all_loads[c][2].wait()
                own_terms(0, c)
            level_event(k - 1, c)
            if c == 0 and k < LEVELS:
                hear(k)
            if k < LEVELS:
                level_copy(k, c).start()
                own_terms(k, c)
        elif event[0] == "a":
            if event[1] == 0:
                told()
            a2a_event(event[1])
        elif event[0] == "p":
            root_copy.start()
            prepare_perm()
            prepare_pick()
        else:
            root_event(event[1])
    for k in range(LEVELS):
        for c in range(CHUNKS):
            level_copy(k, c).wait_send()
    for g in range(len(GROUPS)):
        a2a_bytes(g, N_ORDER - 1).wait_send()
    for copy in (pick_copy, part_copy, coef_copy):
        copy.wait()


def finish_kernel(part_hbm, coef_hbm, pick_hbm, out_hbm, part, coef_t, pick, out, in_sem, out_sem):
    copies = [
        pltpu.make_async_copy(coef_hbm, coef_t, in_sem.at[0]),
        pltpu.make_async_copy(pick_hbm, pick, in_sem.at[1]),
        pltpu.make_async_copy(part_hbm, part, in_sem.at[2]),
    ]
    for copy in copies:
        copy.start()
    degree = lax.axis_index("lat") * 128 + lax.broadcasted_iota(I32, (128, 512), 0)
    window = DEGREES // 512 * lax.broadcasted_iota(I32, (128, 512), 1)
    alive = degree >= window
    for copy in copies:
        copy.wait()
    natural = jnp.dot(coef_t[...].reshape(512, 128), pick[...], preferred_element_type=F32)
    out_copies = []
    for cc in range(4):
        rows = slice(cc * 128, (cc + 1) * 128)
        total = part[rows].astype(F32) + natural[rows]
        out[cc] = jnp.where(alive, total, 0.0).astype(BF16)
        copy = pltpu.make_async_copy(out.at[cc], out_hbm.at[cc // 2, cc % 2], out_sem.at[cc])
        copy.start()
        out_copies.append(copy)
    for copy in out_copies:
        copy.wait()


def per_device(
    fourier, quad_weights, leaf_basis, level_factors, sparsity, root_basis, order_of_slot
):
    anywhere = pl.BlockSpec(memory_space=pl.ANY)
    vmem = pltpu.VMEM
    parts = pl.pallas_call(
        kernel,
        out_shape=[
            jax.ShapeDtypeStruct((512, 512), BF16),
            jax.ShapeDtypeStruct((4, 128, 128), BF16),
            jax.ShapeDtypeStruct((128, 512), BF16),
        ],
        in_specs=[anywhere] * 7,
        out_specs=[anywhere] * 3,
        scratch_shapes=[
            vmem((SLOTS, 64, 128), BF16),
            vmem((1, 128), F32),
            vmem((SLOTS, 64, 128), BF16),
            vmem((SLOTS, LEVELS, 2, 64, 64), BF16),
            pltpu.SMEM((LEVELS, 1, SLOTS), I32),
            vmem((512, 64, 128), BF16),
            vmem((4, 128), I32),
            vmem((LEVELS + 1, CHUNKS, 2, RANK, 128), BF16),
            vmem((LEVELS, CHUNKS, 2, RANK, 128), BF16),
            vmem((LEVELS, CHUNKS, 2, RANK, 128), F32),
            vmem((256, 256), BF16),
            vmem((len(GROUPS), N_ORDER, 16, 128), BF16),
            vmem((len(GROUPS), N_ORDER, 16, 128), BF16),
            vmem((512, 128), F32),
            vmem((512, 512), BF16),
            vmem((512, 128), F32),
            vmem((4, 128, 512), BF16),
            vmem((512, 512), BF16),
            pltpu.SemaphoreType.DMA((3, CHUNKS)),
            pltpu.SemaphoreType.DMA((3,)),
            pltpu.SemaphoreType.DMA,
            pltpu.SemaphoreType.DMA((3,)),
            pltpu.SemaphoreType.DMA((LEVELS, CHUNKS)),
            pltpu.SemaphoreType.DMA((LEVELS, CHUNKS)),
            pltpu.SemaphoreType.DMA((len(GROUPS),)),
            pltpu.SemaphoreType.DMA((len(GROUPS), 2)),
            pltpu.SemaphoreType.REGULAR((LEVELS,)),
            pltpu.SemaphoreType.REGULAR((4,)),
            pltpu.SemaphoreType.REGULAR((4,)),
            pltpu.SemaphoreType.REGULAR,
        ],
        compiler_params=pltpu.CompilerParams(
            collective_id=0, has_side_effects=True, vmem_limit_bytes=60 * 1024 * 1024
        ),
        cost_estimate=pl.CostEstimate(
            flops=2 * 10**9, bytes_accessed=15 * 10**6, transcendentals=0
        ),
    )(
        fourier,
        quad_weights.reshape(1, 128),
        leaf_basis,
        level_factors,
        sparsity.transpose(1, 2, 0),
        root_basis,
        order_of_slot.reshape(4, 128),
    )
    return pl.pallas_call(
        finish_kernel,
        out_shape=jax.ShapeDtypeStruct((2, 2, 128, 512), BF16),
        in_specs=[anywhere] * 3,
        out_specs=anywhere,
        scratch_shapes=[
            vmem((512, 512), BF16),
            vmem((4, 128, 128), BF16),
            vmem((128, 512), BF16),
            vmem((4, 128, 512), BF16),
            pltpu.SemaphoreType.DMA((3,)),
            pltpu.SemaphoreType.DMA((4,)),
        ],
        compiler_params=pltpu.CompilerParams(vmem_limit_bytes=60 * 1024 * 1024),
        cost_estimate=pl.CostEstimate(
            flops=2**26, bytes_accessed=5 * 2**18, transcendentals=0
        ),
    )(*parts)


def solution(mesh):
    return jax.shard_map(
        per_device,
        mesh=mesh,
        in_specs=(
            P("order", None, "lat"),
            P("lat"),
            P("order", None, "lat"),
            P("order", None, None, "lat", None, None),
            P("order", None, "lat"),
            P(None, None, "lat"),
            P(),
        ),
        out_specs=P("order", None, "lat", None),
        check_vma=False,
    )
```

```python
import functools

import jax
import jax.numpy as jnp
from jax import lax
from jax.experimental import pallas as pl
from jax.experimental.pallas import tpu as pltpu
from jax.sharding import PartitionSpec as P

DEGREES = 2048
MESH = pl.DeviceIdType.MESH
BF16 = jnp.bfloat16
F32 = jnp.float32
I32 = jnp.int32

SLOTS = 32
CHUNK = 4
CHUNKS = SLOTS // CHUNK
LEVELS = 4
GROUPS = ((0, 1), (2, 3), (4, 5), (6,), (7,))
LAST = len(GROUPS) - 1
N_ORDER = 16
RANK = 64


HOPS = [(0, 1, 2, 1)[k >> 2] + (0, 1, 2, 1)[k & 3] for k in range(N_ORDER)]
NEAR = [k for k in range(1, N_ORDER) if HOPS[k] <= 2]
FAR = [k for k in range(1, N_ORDER) if HOPS[k] > 2]


def schedule():
    keyed = []
    for c in range(CHUNKS):
        keyed.append((c * 1.0, 0, ("s", 0, c)))
        keyed.append((c * 1.0 + 2.5, 1, ("s", 1, c)))
        keyed.append((c * 1.5 + 5.5, 2, ("s", 2, c)))
        keyed.append((c * 2.0 + 12.0, 3, ("s", 3, c)))
        keyed.append((c * 2.0 + 15.65, 4, ("d", c)))
        keyed.append((c * 2.0 + 19.5, 4, ("s", 4, c)))
    for g, chunks in enumerate(GROUPS):
        keyed.append((chunks[-1] * 2.0 + 19.6, 5, ("a", g)))
        keyed.append((999 + g, 6, ("r", g)))
    keyed.append((8.1, 7, ("p",)))
    return [event for _, _, event in sorted(keyed)]


ROUNDS = [("s", 2, 0), ("s", 2, 2), ("s", 3, 0)]


def kernel(
    four_hbm, quad_hbm, leaf_hbm, fac_hbm, spars_hbm, root_hbm, order_hbm, part_hbm, coef_hbm, pick_hbm,
    four, quad, leaf, fac, spars, root, order,
    state, partner, own, perm, send_buf, recv_buf, order_col, pick, coef, coef_t, part,
    in_sem, small_sem, root_sem, out_sem, send_sem, recv_sem, a2a_send_sem, a2a_recv_sem, round_sem,
):
    me_o = lax.axis_index("order")
    me_l = lax.axis_index("lat")
    peers = [me_l ^ (1 << k) for k in range(LEVELS)]

    def loads(c):
        span = pl.ds(c * CHUNK, CHUNK)
        return [
            pltpu.make_async_copy(four_hbm.at[span], four.at[span], in_sem.at[0, c]),
            pltpu.make_async_copy(leaf_hbm.at[span], leaf.at[span], in_sem.at[1, c]),
            pltpu.make_async_copy(fac_hbm.at[span, :, :, 0], fac.at[span], in_sem.at[2, c]),
        ]

    small = [
        pltpu.make_async_copy(quad_hbm, quad, small_sem.at[0]),
        pltpu.make_async_copy(spars_hbm, spars, small_sem.at[1]),
        pltpu.make_async_copy(order_hbm, order, small_sem.at[2]),
    ]
    root_copy = pltpu.make_async_copy(root_hbm, root, root_sem)
    all_loads = [loads(c) for c in range(CHUNKS)]
    for copy in (all_loads[0][0], all_loads[0][1], small[0]):
        copy.start()

    x, y = me_o // 4, lax.rem(me_o, 4)
    z, core = me_l // 2, lax.rem(me_l, 2)

    def around(axis):
        places = []
        for step in (1, -1):
            if axis == "x":
                places.append((lax.rem(x + step + 4, 4) * 4 + y, me_l))
            elif axis == "y":
                places.append((x * 4 + lax.rem(y + step + 4, 4), me_l))
            else:
                places.append((me_o, lax.rem(z + step + 8, 8) * 2 + core))
        return places

    barrier = pltpu.get_barrier_semaphore()
    neighbours = [(me_o, peers[0])] + around("x") + around("y") + around("z")
    for place in neighbours:
        pl.semaphore_signal(barrier, inc=1, device_id=place, device_id_type=MESH)

    def tell(n):
        for place in around("y" if n == 0 else "x") + around("z"):
            pl.semaphore_signal(round_sem.at[n], inc=1, device_id=place, device_id_type=MESH)

    def hear(n):
        pl.semaphore_wait(round_sem.at[n], 4)

    for c in range(1, CHUNKS):
        for copy in all_loads[c][:2]:
            copy.start()
    for copy in small[1:]:
        copy.start()
    for c in range(CHUNKS):
        all_loads[c][2].start()

    def level_copy(k, c):
        return pltpu.make_async_remote_copy(
            src_ref=state.at[k, c],
            dst_ref=partner.at[k, c],
            send_sem=send_sem.at[k, c],
            recv_sem=recv_sem.at[k, c],
            device_id=(me_o, peers[k]),
            device_id_type=MESH,
        )

    def a2a_copy(g, k):
        return pltpu.make_async_remote_copy(
            src_ref=send_buf.at[g, me_o ^ k],
            dst_ref=recv_buf.at[g, k],
            send_sem=a2a_send_sem.at[g],
            recv_sem=a2a_recv_sem.at[g, int(g == LAST and k in FAR)],
            device_id=(me_o ^ k, me_l),
            device_id_type=MESH,
        )

    def a2a_bytes(g, count, far=0):
        return pltpu.make_async_remote_copy(
            src_ref=send_buf.at[g, pl.ds(0, count)],
            dst_ref=recv_buf.at[g, pl.ds(0, count)],
            send_sem=a2a_send_sem.at[g],
            recv_sem=a2a_recv_sem.at[g, far],
            device_id=(me_o ^ 1, me_l),
            device_id_type=MESH,
        )

    low = lax.broadcasted_iota(I32, (RANK, 128), 1) < RANK

    def both(a, b):
        return jnp.concatenate([a, b], axis=0)

    def diagonal(product):
        return jnp.where(low, product[:RANK], product[RANK:])

    def own_terms(k, c):
        for h in range(2):
            s0, s1 = c * CHUNK + h, c * CHUNK + 2 + h
            a = both(fac[s0, k, 0], fac[s1, k, 0])
            own[k, c, h] = diagonal(jnp.dot(a, state[k, c, h], preferred_element_type=F32))

    def start_event(c):
        for copy in all_loads[c][:2]:
            copy.wait()
        w = quad[...]
        for h in range(2):
            s0, s1 = c * CHUNK + h, c * CHUNK + 2 + h
            weighted = both(
                (four[s0].astype(F32) * w).astype(BF16), (four[s1].astype(F32) * w).astype(BF16)
            )
            basis = both(leaf[s0], leaf[s1])
            product = lax.dot_general(
                basis, weighted, (((1,), (1,)), ((), ())), preferred_element_type=F32
            )
            state[0, c, h] = diagonal(product).astype(BF16)

    def level_event(k, c):
        level_copy(k, c).wait_recv()
        for h in range(2):
            s0, s1 = c * CHUNK + h, c * CHUNK + 2 + h
            b = both(fac[s0, k, 1], fac[s1, k, 1])
            cross = diagonal(jnp.dot(b, partner[k, c, h], preferred_element_type=F32))
            present = jnp.where(low, spars[k, 0, s0], spars[k, 0, s1]).astype(F32)
            state[k + 1, c, h] = (own[k, c, h] + present * cross).astype(BF16)

    def a2a_event(g):
        x = [state[LEVELS, c].reshape(2 * RANK, 128) for c in GROUPS[g]]
        packed = lax.dot_general(
            perm[:, : 128 * len(x)],
            jnp.concatenate(x, axis=1),
            (((1,), (1,)), ((), ())),
            preferred_element_type=F32,
        ).astype(BF16)
        send_buf[g] = packed.reshape(N_ORDER, 16, 128)
        for k in sorted(NEAR + FAR, key=lambda k: -HOPS[k]):
            a2a_copy(g, k).start()
        recv_buf[g, 0] = send_buf[g, me_o]

    def prepare_perm():
        row = lax.broadcasted_iota(I32, (256, 256), 0)
        col = lax.broadcasted_iota(I32, (256, 256), 1)
        target = (row & 3) * 64 + (row >> 4) * 4 + ((row >> 2) & 3)
        perm[...] = (col == target).astype(F32).astype(BF16)

    def prepare_pick():
        small[2].wait()
        orders = order[...].astype(F32)
        for i in range(4):
            wide = jnp.broadcast_to(orders[i : i + 1], (128, 128))
            order_col[pl.ds(i * 128, 128)] = wide.T
        window = lax.broadcasted_iota(I32, (16, 512), 1).astype(F32)
        for g in range(SLOTS // 8):
            for q in range(4):
                for h in range(2):
                    col = order_col[pl.ds(8 * g + 2 * q + h, 16, stride=SLOTS), :]
                    wide = jnp.concatenate([col] * 4, axis=1)
                    row = g * 128 + q * 32 + h * 16
                    pick[pl.ds(row, 16)] = (wide == window).astype(F32).astype(BF16)
        pick_copy.start()

    def root_event(g):
        if g == 0:
            root_copy.wait()
        pair = len(GROUPS[g]) == 2
        row = lax.broadcasted_iota(I32, (32, 256), 0)
        col = lax.broadcasted_iota(I32, (32, 256), 1)
        keep = ((row >> 4) == ((col >> 6) & 1)) & ((row & 1) == (col >> 7))
        keep = keep.astype(F32).astype(BF16)
        first = (lax.broadcasted_iota(I32, (32, 128), 0) & 2) == 0

        def one(k):
            source = me_o ^ k
            r = recv_buf[g, k]
            r2 = jnp.concatenate([r, r], axis=1)
            lhs = jnp.concatenate([r2, r2], axis=0) * keep
            base = source * SLOTS + GROUPS[g][0] * CHUNK
            w = root[pl.ds(base, 4)].reshape(256, 128)
            if pair:
                w = jnp.concatenate([w, root[pl.ds(base + 4, 4)].reshape(256, 128)], axis=1)
            product = jnp.dot(lhs, w, preferred_element_type=F32)
            if pair:
                product = jnp.where(first, product[:, :128], product[:, 128:])
            coef[pl.ds(pl.multiple_of(source * 32, 32), 32)] = product

        if g == LAST:
            one(0)
            a2a_bytes(g, len(NEAR), 0).wait_recv()
            for k in NEAR:
                one(k)
            a2a_bytes(g, len(FAR), 1).wait_recv()
            for k in FAR:
                one(k)
        else:
            a2a_bytes(g, N_ORDER - 1).wait_recv()

            def body(k, carry):
                one(k)
                return carry

            lax.fori_loop(0, N_ORDER, body, 0, unroll=4)
        width = 128 if pair else 64
        lanes = pl.ds(GROUPS[g][0] * 64, width)
        for cc in range(4):
            parts = []
            for q in range(width // 32):
                for h in range(2):
                    parts.append(coef[pl.ds(h * 16 + cc * 4 + q, 16, stride=32), :])
            coef_t[cc, :, lanes] = jnp.concatenate(parts, axis=0).T.astype(BF16)
        if g == 2:
            part[...] = jnp.dot(
                coef_t[:, :, :384].reshape(512, 384), pick[:384], preferred_element_type=F32
            ).astype(BF16)
            part_copy.start()
        if g == LAST:
            coef_copy.start()

    coef_copy = pltpu.make_async_copy(coef_t.at[:, :, pl.ds(384, 128)], coef_hbm, out_sem.at[0])
    pick_copy = pltpu.make_async_copy(pick.at[pl.ds(384, 128)], pick_hbm, out_sem.at[1])
    part_copy = pltpu.make_async_copy(part, part_hbm, out_sem.at[2])

    small[0].wait()
    passed = False
    hold = (z == 1) | (z == 2)
    for event in schedule():
        if event[0] == "s" and event[1] == 0:
            c = event[2]
            start_event(c)
            if not passed:
                pl.semaphore_wait(barrier, len(neighbours))
                passed = True
            level_copy(0, c).start()
            if c == 0:
                tell(0)
        elif event[0] == "s":
            _, k, c = event
            if event == ("s", 1, 0):
                small[1].wait()
            if event in ROUNDS:
                hear(ROUNDS.index(event))
                if event != ROUNDS[-1]:
                    tell(ROUNDS.index(event) + 1)
            if k == 1:
                all_loads[c][2].wait()
                own_terms(0, c)
            level_event(k - 1, c)
            if k == LEVELS - 1:
                pl.when(jnp.logical_not(hold))(level_copy(k, c).start)
                own_terms(k, c)
            elif k < LEVELS:
                level_copy(k, c).start()
                own_terms(k, c)
        elif event[0] == "d":
            pl.when(hold)(level_copy(LEVELS - 1, event[1]).start)
        elif event[0] == "a":
            a2a_event(event[1])
        elif event[0] == "p":
            root_copy.start()
            prepare_perm()
            prepare_pick()
        else:
            root_event(event[1])
    for k in range(LEVELS):
        for c in range(CHUNKS):
            level_copy(k, c).wait_send()
    for g in range(len(GROUPS)):
        a2a_bytes(g, N_ORDER - 1).wait_send()
    for copy in (pick_copy, part_copy, coef_copy):
        copy.wait()


def finish_kernel(part_hbm, coef_hbm, pick_hbm, out_hbm, part, coef_t, pick, out, in_sem, out_sem):
    copies = [
        pltpu.make_async_copy(coef_hbm, coef_t, in_sem.at[0]),
        pltpu.make_async_copy(pick_hbm, pick, in_sem.at[1]),
        pltpu.make_async_copy(part_hbm, part, in_sem.at[2]),
    ]
    for copy in copies:
        copy.start()
    degree = lax.axis_index("lat") * 128 + lax.broadcasted_iota(I32, (128, 512), 0)
    window = DEGREES // 512 * lax.broadcasted_iota(I32, (128, 512), 1)
    alive = degree >= window
    for copy in copies:
        copy.wait()
    natural = jnp.dot(coef_t[...].reshape(512, 128), pick[...], preferred_element_type=F32)
    out_copies = []
    for cc in range(4):
        rows = slice(cc * 128, (cc + 1) * 128)
        total = part[rows].astype(F32) + natural[rows]
        out[cc] = jnp.where(alive, total, 0.0).astype(BF16)
        copy = pltpu.make_async_copy(out.at[cc], out_hbm.at[cc // 2, cc % 2], out_sem.at[cc])
        copy.start()
        out_copies.append(copy)
    for copy in out_copies:
        copy.wait()


def per_device(
    fourier, quad_weights, leaf_basis, level_factors, sparsity, root_basis, order_of_slot
):
    anywhere = pl.BlockSpec(memory_space=pl.ANY)
    vmem = pltpu.VMEM
    parts = pl.pallas_call(
        kernel,
        out_shape=[
            jax.ShapeDtypeStruct((512, 512), BF16),
            jax.ShapeDtypeStruct((4, 128, 128), BF16),
            jax.ShapeDtypeStruct((128, 512), BF16),
        ],
        in_specs=[anywhere] * 7,
        out_specs=[anywhere] * 3,
        scratch_shapes=[
            vmem((SLOTS, 64, 128), BF16),
            vmem((1, 128), F32),
            vmem((SLOTS, 64, 128), BF16),
            vmem((SLOTS, LEVELS, 2, 64, 64), BF16),
            pltpu.SMEM((LEVELS, 1, SLOTS), I32),
            vmem((512, 64, 128), BF16),
            vmem((4, 128), I32),
            vmem((LEVELS + 1, CHUNKS, 2, RANK, 128), BF16),
            vmem((LEVELS, CHUNKS, 2, RANK, 128), BF16),
            vmem((LEVELS, CHUNKS, 2, RANK, 128), F32),
            vmem((256, 256), BF16),
            vmem((len(GROUPS), N_ORDER, 16, 128), BF16),
            vmem((len(GROUPS), N_ORDER, 16, 128), BF16),
            vmem((512, 128), F32),
            vmem((512, 512), BF16),
            vmem((512, 128), F32),
            vmem((4, 128, 512), BF16),
            vmem((512, 512), BF16),
            pltpu.SemaphoreType.DMA((3, CHUNKS)),
            pltpu.SemaphoreType.DMA((3,)),
            pltpu.SemaphoreType.DMA,
            pltpu.SemaphoreType.DMA((3,)),
            pltpu.SemaphoreType.DMA((LEVELS, CHUNKS)),
            pltpu.SemaphoreType.DMA((LEVELS, CHUNKS)),
            pltpu.SemaphoreType.DMA((len(GROUPS),)),
            pltpu.SemaphoreType.DMA((len(GROUPS), 2)),
            pltpu.SemaphoreType.REGULAR((3,)),
        ],
        compiler_params=pltpu.CompilerParams(
            collective_id=0, has_side_effects=True, vmem_limit_bytes=60 * 1024 * 1024
        ),
        cost_estimate=pl.CostEstimate(
            flops=2 * 10**9, bytes_accessed=15 * 10**6, transcendentals=0
        ),
    )(
        fourier,
        quad_weights.reshape(1, 128),
        leaf_basis,
        level_factors,
        sparsity.transpose(1, 2, 0),
        root_basis,
        order_of_slot.reshape(4, 128),
    )
    return pl.pallas_call(
        finish_kernel,
        out_shape=jax.ShapeDtypeStruct((2, 2, 128, 512), BF16),
        in_specs=[anywhere] * 3,
        out_specs=anywhere,
        scratch_shapes=[
            vmem((512, 512), BF16),
            vmem((4, 128, 128), BF16),
            vmem((128, 512), BF16),
            vmem((4, 128, 512), BF16),
            pltpu.SemaphoreType.DMA((3,)),
            pltpu.SemaphoreType.DMA((4,)),
        ],
        compiler_params=pltpu.CompilerParams(vmem_limit_bytes=60 * 1024 * 1024),
        cost_estimate=pl.CostEstimate(
            flops=2**26, bytes_accessed=5 * 2**18, transcendentals=0
        ),
    )(*parts)


def solution(mesh):
    return jax.shard_map(
        per_device,
        mesh=mesh,
        in_specs=(
            P("order", None, "lat"),
            P("lat"),
            P("order", None, "lat"),
            P("order", None, None, "lat", None, None),
            P("order", None, "lat"),
            P(None, None, "lat"),
            P(),
        ),
        out_specs=P("order", None, "lat", None),
        check_vma=False,
    )
```

```python
import functools

import jax
import jax.numpy as jnp
from jax import lax
from jax.experimental import pallas as pl
from jax.experimental.pallas import tpu as pltpu
from jax.sharding import PartitionSpec as P

DEGREES = 2048
MESH = pl.DeviceIdType.MESH
BF16 = jnp.bfloat16
F32 = jnp.float32
I32 = jnp.int32

SLOTS = 32
CHUNK = 4
CHUNKS = SLOTS // CHUNK
LEVELS = 4
GROUPS = ((0, 1), (2, 3), (4, 5), (6,), (7,))
LAST = len(GROUPS) - 1
N_ORDER = 16
RANK = 64


HOPS = [(0, 1, 2, 1)[k >> 2] + (0, 1, 2, 1)[k & 3] for k in range(N_ORDER)]
NEAR = [k for k in range(1, N_ORDER) if HOPS[k] <= 2]
FAR = [k for k in range(1, N_ORDER) if HOPS[k] > 2]


def schedule():
    keyed = []
    for c in range(CHUNKS):
        keyed.append((c * 1.0, 0, ("s", 0, c)))
        keyed.append((c * 1.0 + 2.5, 1, ("s", 1, c)))
        keyed.append((c * 1.25 + 5.5, 2, ("s", 2, c)))
        keyed.append((c * 2.0 + 12.0, 3, ("s", 3, c)))
        keyed.append((c * 2.0 + 15.65, 4, ("d", c)))
        keyed.append((c * 2.0 + 19.5, 4, ("s", 4, c)))
    for g, chunks in enumerate(GROUPS):
        keyed.append((chunks[-1] * 2.0 + 19.6, 5, ("a", g)))
        keyed.append((999 + g, 6, ("r", g)))
    keyed.append((8.1, 7, ("p",)))
    return [event for _, _, event in sorted(keyed)]


ROUNDS = [("s", 2, 0), ("s", 2, 2), ("s", 3, 0)]


def kernel(
    four_hbm, quad_hbm, leaf_hbm, fac_hbm, spars_hbm, root_hbm, order_hbm, part_hbm, coef_hbm, pick_hbm,
    four, quad, leaf, fac, spars, root, order,
    state, partner, own, perm, send_buf, recv_buf, order_col, pick, coef, coef_t, part,
    in_sem, small_sem, root_sem, out_sem, send_sem, recv_sem, a2a_send_sem, a2a_recv_sem, round_sem,
):
    me_o = lax.axis_index("order")
    me_l = lax.axis_index("lat")
    peers = [me_l ^ (1 << k) for k in range(LEVELS)]

    def loads(c):
        span = pl.ds(c * CHUNK, CHUNK)
        return [
            pltpu.make_async_copy(four_hbm.at[span], four.at[span], in_sem.at[0, c]),
            pltpu.make_async_copy(leaf_hbm.at[span], leaf.at[span], in_sem.at[1, c]),
            pltpu.make_async_copy(fac_hbm.at[span, :, :, 0], fac.at[span], in_sem.at[2, c]),
        ]

    small = [
        pltpu.make_async_copy(quad_hbm, quad, small_sem.at[0]),
        pltpu.make_async_copy(spars_hbm, spars, small_sem.at[1]),
        pltpu.make_async_copy(order_hbm, order, small_sem.at[2]),
    ]
    root_copy = pltpu.make_async_copy(root_hbm, root, root_sem)
    all_loads = [loads(c) for c in range(CHUNKS)]
    for copy in (all_loads[0][0], all_loads[0][1], small[0]):
        copy.start()

    x, y = me_o // 4, lax.rem(me_o, 4)
    z, core = me_l // 2, lax.rem(me_l, 2)

    def around(axis):
        places = []
        for step in (1, -1):
            if axis == "x":
                places.append((lax.rem(x + step + 4, 4) * 4 + y, me_l))
            elif axis == "y":
                places.append((x * 4 + lax.rem(y + step + 4, 4), me_l))
            else:
                places.append((me_o, lax.rem(z + step + 8, 8) * 2 + core))
        return places

    barrier = pltpu.get_barrier_semaphore()
    neighbours = [(me_o, peers[0])] + around("x") + around("y") + around("z")
    for place in neighbours:
        pl.semaphore_signal(barrier, inc=1, device_id=place, device_id_type=MESH)

    def tell(n):
        for place in around("y" if n == 0 else "x") + around("z"):
            pl.semaphore_signal(round_sem.at[n], inc=1, device_id=place, device_id_type=MESH)

    def hear(n):
        pl.semaphore_wait(round_sem.at[n], 4)

    for c in range(1, CHUNKS):
        for copy in all_loads[c][:2]:
            copy.start()
    for copy in small[1:]:
        copy.start()
    for c in range(CHUNKS):
        all_loads[c][2].start()

    def level_copy(k, c):
        return pltpu.make_async_remote_copy(
            src_ref=state.at[k, c],
            dst_ref=partner.at[k, c],
            send_sem=send_sem.at[k, c],
            recv_sem=recv_sem.at[k, c],
            device_id=(me_o, peers[k]),
            device_id_type=MESH,
        )

    def a2a_copy(g, k):
        return pltpu.make_async_remote_copy(
            src_ref=send_buf.at[g, me_o ^ k],
            dst_ref=recv_buf.at[g, k],
            send_sem=a2a_send_sem.at[g],
            recv_sem=a2a_recv_sem.at[g, int(g == LAST and k in FAR)],
            device_id=(me_o ^ k, me_l),
            device_id_type=MESH,
        )

    def a2a_bytes(g, count, far=0):
        return pltpu.make_async_remote_copy(
            src_ref=send_buf.at[g, pl.ds(0, count)],
            dst_ref=recv_buf.at[g, pl.ds(0, count)],
            send_sem=a2a_send_sem.at[g],
            recv_sem=a2a_recv_sem.at[g, far],
            device_id=(me_o ^ 1, me_l),
            device_id_type=MESH,
        )

    low = lax.broadcasted_iota(I32, (RANK, 128), 1) < RANK

    def both(a, b):
        return jnp.concatenate([a, b], axis=0)

    def diagonal(product):
        return jnp.where(low, product[:RANK], product[RANK:])

    def own_terms(k, c):
        for h in range(2):
            s0, s1 = c * CHUNK + h, c * CHUNK + 2 + h
            a = both(fac[s0, k, 0], fac[s1, k, 0])
            own[k, c, h] = diagonal(jnp.dot(a, state[k, c, h], preferred_element_type=F32))

    def start_event(c):
        for copy in all_loads[c][:2]:
            copy.wait()
        w = quad[...]
        for h in range(2):
            s0, s1 = c * CHUNK + h, c * CHUNK + 2 + h
            weighted = both(
                (four[s0].astype(F32) * w).astype(BF16), (four[s1].astype(F32) * w).astype(BF16)
            )
            basis = both(leaf[s0], leaf[s1])
            product = lax.dot_general(
                basis, weighted, (((1,), (1,)), ((), ())), preferred_element_type=F32
            )
            state[0, c, h] = diagonal(product).astype(BF16)

    def level_event(k, c):
        level_copy(k, c).wait_recv()
        for h in range(2):
            s0, s1 = c * CHUNK + h, c * CHUNK + 2 + h
            b = both(fac[s0, k, 1], fac[s1, k, 1])
            cross = diagonal(jnp.dot(b, partner[k, c, h], preferred_element_type=F32))
            present = jnp.where(low, spars[k, 0, s0], spars[k, 0, s1]).astype(F32)
            state[k + 1, c, h] = (own[k, c, h] + present * cross).astype(BF16)

    def a2a_event(g):
        x = [state[LEVELS, c].reshape(2 * RANK, 128) for c in GROUPS[g]]
        packed = lax.dot_general(
            perm[:, : 128 * len(x)],
            jnp.concatenate(x, axis=1),
            (((1,), (1,)), ((), ())),
            preferred_element_type=F32,
        ).astype(BF16)
        send_buf[g] = packed.reshape(N_ORDER, 16, 128)
        for k in sorted(NEAR + FAR, key=lambda k: -HOPS[k]):
            a2a_copy(g, k).start()
        recv_buf[g, 0] = send_buf[g, me_o]

    def prepare_perm():
        row = lax.broadcasted_iota(I32, (256, 256), 0)
        col = lax.broadcasted_iota(I32, (256, 256), 1)
        target = (row & 3) * 64 + (row >> 4) * 4 + ((row >> 2) & 3)
        perm[...] = (col == target).astype(F32).astype(BF16)

    def prepare_pick():
        small[2].wait()
        orders = order[...].astype(F32)
        for i in range(4):
            wide = jnp.broadcast_to(orders[i : i + 1], (128, 128))
            order_col[pl.ds(i * 128, 128)] = wide.T
        window = lax.broadcasted_iota(I32, (16, 512), 1).astype(F32)
        for g in range(SLOTS // 8):
            for q in range(4):
                for h in range(2):
                    col = order_col[pl.ds(8 * g + 2 * q + h, 16, stride=SLOTS), :]
                    wide = jnp.concatenate([col] * 4, axis=1)
                    row = g * 128 + q * 32 + h * 16
                    pick[pl.ds(row, 16)] = (wide == window).astype(F32).astype(BF16)
        pick_copy.start()

    def root_event(g):
        if g == 0:
            root_copy.wait()
        pair = len(GROUPS[g]) == 2
        row = lax.broadcasted_iota(I32, (32, 256), 0)
        col = lax.broadcasted_iota(I32, (32, 256), 1)
        keep = ((row >> 4) == ((col >> 6) & 1)) & ((row & 1) == (col >> 7))
        keep = keep.astype(F32).astype(BF16)
        first = (lax.broadcasted_iota(I32, (32, 128), 0) & 2) == 0

        def one(k):
            source = me_o ^ k
            r = recv_buf[g, k]
            r2 = jnp.concatenate([r, r], axis=1)
            lhs = jnp.concatenate([r2, r2], axis=0) * keep
            base = source * SLOTS + GROUPS[g][0] * CHUNK
            w = root[pl.ds(base, 4)].reshape(256, 128)
            if pair:
                w = jnp.concatenate([w, root[pl.ds(base + 4, 4)].reshape(256, 128)], axis=1)
            product = jnp.dot(lhs, w, preferred_element_type=F32)
            if pair:
                product = jnp.where(first, product[:, :128], product[:, 128:])
            coef[pl.ds(pl.multiple_of(source * 32, 32), 32)] = product

        if g == LAST:
            one(0)
            a2a_bytes(g, len(NEAR), 0).wait_recv()
            for k in NEAR:
                one(k)
            a2a_bytes(g, len(FAR), 1).wait_recv()
            for k in FAR:
                one(k)
        else:
            a2a_bytes(g, N_ORDER - 1).wait_recv()

            def body(k, carry):
                one(k)
                return carry

            lax.fori_loop(0, N_ORDER, body, 0, unroll=4)
        width = 128 if pair else 64
        lanes = pl.ds(GROUPS[g][0] * 64, width)
        for cc in range(4):
            parts = []
            for q in range(width // 32):
                for h in range(2):
                    parts.append(coef[pl.ds(h * 16 + cc * 4 + q, 16, stride=32), :])
            coef_t[cc, :, lanes] = jnp.concatenate(parts, axis=0).T.astype(BF16)
        if g == 2:
            part[...] = jnp.dot(
                coef_t[:, :, :384].reshape(512, 384), pick[:384], preferred_element_type=F32
            ).astype(BF16)
            part_copy.start()
        if g == LAST:
            coef_copy.start()

    coef_copy = pltpu.make_async_copy(coef_t.at[:, :, pl.ds(384, 128)], coef_hbm, out_sem.at[0])
    pick_copy = pltpu.make_async_copy(pick.at[pl.ds(384, 128)], pick_hbm, out_sem.at[1])
    part_copy = pltpu.make_async_copy(part, part_hbm, out_sem.at[2])

    small[0].wait()
    passed = False
    hold = (z == 1) | (z == 2)
    for event in schedule():
        if event[0] == "s" and event[1] == 0:
            c = event[2]
            start_event(c)
            if not passed:
                pl.semaphore_wait(barrier, len(neighbours))
                passed = True
            level_copy(0, c).start()
            if c == 0:
                tell(0)
        elif event[0] == "s":
            _, k, c = event
            if event == ("s", 1, 0):
                small[1].wait()
            if event in ROUNDS:
                hear(ROUNDS.index(event))
                if event != ROUNDS[-1]:
                    tell(ROUNDS.index(event) + 1)
            if k == 1:
                all_loads[c][2].wait()
                own_terms(0, c)
            level_event(k - 1, c)
            if k == LEVELS - 1:
                pl.when(jnp.logical_not(hold))(level_copy(k, c).start)
                own_terms(k, c)
            elif k < LEVELS:
                level_copy(k, c).start()
                own_terms(k, c)
        elif event[0] == "d":
            pl.when(hold)(level_copy(LEVELS - 1, event[1]).start)
        elif event[0] == "a":
            a2a_event(event[1])
        elif event[0] == "p":
            root_copy.start()
            prepare_perm()
            prepare_pick()
        else:
            root_event(event[1])
    for k in range(LEVELS):
        for c in range(CHUNKS):
            level_copy(k, c).wait_send()
    for g in range(len(GROUPS)):
        a2a_bytes(g, N_ORDER - 1).wait_send()
    for copy in (pick_copy, part_copy, coef_copy):
        copy.wait()


def finish_kernel(part_hbm, coef_hbm, pick_hbm, out_hbm, part, coef_t, pick, out, in_sem, out_sem):
    copies = [
        pltpu.make_async_copy(coef_hbm, coef_t, in_sem.at[0]),
        pltpu.make_async_copy(pick_hbm, pick, in_sem.at[1]),
        pltpu.make_async_copy(part_hbm, part, in_sem.at[2]),
    ]
    for copy in copies:
        copy.start()
    degree = lax.axis_index("lat") * 128 + lax.broadcasted_iota(I32, (128, 512), 0)
    window = DEGREES // 512 * lax.broadcasted_iota(I32, (128, 512), 1)
    alive = degree >= window
    for copy in copies:
        copy.wait()
    natural = jnp.dot(coef_t[...].reshape(512, 128), pick[...], preferred_element_type=F32)
    out_copies = []
    for cc in range(4):
        rows = slice(cc * 128, (cc + 1) * 128)
        total = part[rows].astype(F32) + natural[rows]
        out[cc] = jnp.where(alive, total, 0.0).astype(BF16)
        copy = pltpu.make_async_copy(out.at[cc], out_hbm.at[cc // 2, cc % 2], out_sem.at[cc])
        copy.start()
        out_copies.append(copy)
    for copy in out_copies:
        copy.wait()


def per_device(
    fourier, quad_weights, leaf_basis, level_factors, sparsity, root_basis, order_of_slot
):
    anywhere = pl.BlockSpec(memory_space=pl.ANY)
    vmem = pltpu.VMEM
    parts = pl.pallas_call(
        kernel,
        out_shape=[
            jax.ShapeDtypeStruct((512, 512), BF16),
            jax.ShapeDtypeStruct((4, 128, 128), BF16),
            jax.ShapeDtypeStruct((128, 512), BF16),
        ],
        in_specs=[anywhere] * 7,
        out_specs=[anywhere] * 3,
        scratch_shapes=[
            vmem((SLOTS, 64, 128), BF16),
            vmem((1, 128), F32),
            vmem((SLOTS, 64, 128), BF16),
            vmem((SLOTS, LEVELS, 2, 64, 64), BF16),
            pltpu.SMEM((LEVELS, 1, SLOTS), I32),
            vmem((512, 64, 128), BF16),
            vmem((4, 128), I32),
            vmem((LEVELS + 1, CHUNKS, 2, RANK, 128), BF16),
            vmem((LEVELS, CHUNKS, 2, RANK, 128), BF16),
            vmem((LEVELS, CHUNKS, 2, RANK, 128), F32),
            vmem((256, 256), BF16),
            vmem((len(GROUPS), N_ORDER, 16, 128), BF16),
            vmem((len(GROUPS), N_ORDER, 16, 128), BF16),
            vmem((512, 128), F32),
            vmem((512, 512), BF16),
            vmem((512, 128), F32),
            vmem((4, 128, 512), BF16),
            vmem((512, 512), BF16),
            pltpu.SemaphoreType.DMA((3, CHUNKS)),
            pltpu.SemaphoreType.DMA((3,)),
            pltpu.SemaphoreType.DMA,
            pltpu.SemaphoreType.DMA((3,)),
            pltpu.SemaphoreType.DMA((LEVELS, CHUNKS)),
            pltpu.SemaphoreType.DMA((LEVELS, CHUNKS)),
            pltpu.SemaphoreType.DMA((len(GROUPS),)),
            pltpu.SemaphoreType.DMA((len(GROUPS), 2)),
            pltpu.SemaphoreType.REGULAR((3,)),
        ],
        compiler_params=pltpu.CompilerParams(
            collective_id=0, has_side_effects=True, vmem_limit_bytes=60 * 1024 * 1024
        ),
        cost_estimate=pl.CostEstimate(
            flops=2 * 10**9, bytes_accessed=15 * 10**6, transcendentals=0
        ),
    )(
        fourier,
        quad_weights.reshape(1, 128),
        leaf_basis,
        level_factors,
        sparsity.transpose(1, 2, 0),
        root_basis,
        order_of_slot.reshape(4, 128),
    )
    return pl.pallas_call(
        finish_kernel,
        out_shape=jax.ShapeDtypeStruct((2, 2, 128, 512), BF16),
        in_specs=[anywhere] * 3,
        out_specs=anywhere,
        scratch_shapes=[
            vmem((512, 512), BF16),
            vmem((4, 128, 128), BF16),
            vmem((128, 512), BF16),
            vmem((4, 128, 512), BF16),
            pltpu.SemaphoreType.DMA((3,)),
            pltpu.SemaphoreType.DMA((4,)),
        ],
        compiler_params=pltpu.CompilerParams(vmem_limit_bytes=60 * 1024 * 1024),
        cost_estimate=pl.CostEstimate(
            flops=2**26, bytes_accessed=5 * 2**18, transcendentals=0
        ),
    )(*parts)


def solution(mesh):
    return jax.shard_map(
        per_device,
        mesh=mesh,
        in_specs=(
            P("order", None, "lat"),
            P("lat"),
            P("order", None, "lat"),
            P("order", None, None, "lat", None, None),
            P("order", None, "lat"),
            P(None, None, "lat"),
            P(),
        ),
        out_specs=P("order", None, "lat", None),
        check_vma=False,
    )
```

```python
import functools

import jax
import jax.numpy as jnp
from jax import lax
from jax.experimental import pallas as pl
from jax.experimental.pallas import tpu as pltpu
from jax.sharding import PartitionSpec as P

DEGREES = 2048
MESH = pl.DeviceIdType.MESH
BF16 = jnp.bfloat16
F32 = jnp.float32
I32 = jnp.int32

SLOTS = 32
CHUNK = 4
CHUNKS = SLOTS // CHUNK
LEVELS = 4
GROUPS = ((0, 1), (2, 3), (4, 5), (6,), (7,))
LAST = len(GROUPS) - 1
N_ORDER = 16
RANK = 64


HOPS = [(0, 1, 2, 1)[k >> 2] + (0, 1, 2, 1)[k & 3] for k in range(N_ORDER)]
NEAR = [k for k in range(1, N_ORDER) if HOPS[k] <= 2]
FAR = [k for k in range(1, N_ORDER) if HOPS[k] > 2]


def schedule():
    keyed = []
    for c in range(CHUNKS):
        keyed.append((c * 1.0, 0, ("s", 0, c)))
        keyed.append((c * 1.0 + 2.5, 1, ("s", 1, c)))
        keyed.append((c * 1.5 + 5.5, 2, ("s", 2, c)))
        keyed.append((c * 2.0 + 12.0, 3, ("s", 3, c)))
        keyed.append((c * 2.0 + 15.65, 4, ("d", c)))
        keyed.append((c * 2.0 + 19.5, 4, ("s", 4, c)))
    for g, chunks in enumerate(GROUPS):
        keyed.append((chunks[-1] * 2.0 + 19.6, 5, ("a", g)))
        keyed.append((999 + g, 6, ("r", g)))
    keyed.append((8.1, 7, ("p",)))
    return [event for _, _, event in sorted(keyed)]


ROUNDS = [("s", 2, 0), ("s", 2, 2), ("s", 3, 0)]


def kernel(
    four_hbm, quad_hbm, leaf_hbm, fac_hbm, spars_hbm, root_hbm, order_hbm, part_hbm, coef_hbm, pick_hbm,
    four, quad, leaf, fac, spars, root, order,
    state, partner, own, perm, send_buf, recv_buf, order_col, pick, coef, coef_t, part,
    in_sem, small_sem, root_sem, out_sem, send_sem, recv_sem, a2a_send_sem, a2a_recv_sem, round_sem,
):
    me_o = lax.axis_index("order")
    me_l = lax.axis_index("lat")
    peers = [me_l ^ (1 << k) for k in range(LEVELS)]

    def loads(c):
        span = pl.ds(c * CHUNK, CHUNK)
        return [
            pltpu.make_async_copy(four_hbm.at[span], four.at[span], in_sem.at[0, c]),
            pltpu.make_async_copy(leaf_hbm.at[span], leaf.at[span], in_sem.at[1, c]),
            pltpu.make_async_copy(fac_hbm.at[span, :, :, 0], fac.at[span], in_sem.at[2, c]),
        ]

    small = [
        pltpu.make_async_copy(quad_hbm, quad, small_sem.at[0]),
        pltpu.make_async_copy(spars_hbm, spars, small_sem.at[1]),
        pltpu.make_async_copy(order_hbm, order, small_sem.at[2]),
    ]
    root_copy = pltpu.make_async_copy(root_hbm, root, root_sem)
    all_loads = [loads(c) for c in range(CHUNKS)]
    for copy in (all_loads[0][0], all_loads[0][1], small[0]):
        copy.start()

    x, y = me_o // 4, lax.rem(me_o, 4)
    z, core = me_l // 2, lax.rem(me_l, 2)

    def around(axis):
        places = []
        for step in (1, -1):
            if axis == "x":
                places.append((lax.rem(x + step + 4, 4) * 4 + y, me_l))
            elif axis == "y":
                places.append((x * 4 + lax.rem(y + step + 4, 4), me_l))
            else:
                places.append((me_o, lax.rem(z + step + 8, 8) * 2 + core))
        return places

    barrier = pltpu.get_barrier_semaphore()
    neighbours = [(me_o, peers[0])] + around("x") + around("y") + around("z")
    for place in neighbours:
        pl.semaphore_signal(barrier, inc=1, device_id=place, device_id_type=MESH)

    def tell(n):
        for place in around("y" if n == 0 else "x") + around("z"):
            pl.semaphore_signal(round_sem.at[n], inc=1, device_id=place, device_id_type=MESH)

    def hear(n):
        pl.semaphore_wait(round_sem.at[n], 4)

    for c in range(1, CHUNKS):
        for copy in all_loads[c][:2]:
            copy.start()
    for copy in small[1:]:
        copy.start()
    for c in range(CHUNKS):
        all_loads[c][2].start()

    def level_copy(k, c):
        return pltpu.make_async_remote_copy(
            src_ref=state.at[k, c],
            dst_ref=partner.at[k, c],
            send_sem=send_sem.at[k, c],
            recv_sem=recv_sem.at[k, c],
            device_id=(me_o, peers[k]),
            device_id_type=MESH,
        )

    def a2a_copy(g, k):
        return pltpu.make_async_remote_copy(
            src_ref=send_buf.at[g, me_o ^ k],
            dst_ref=recv_buf.at[g, k],
            send_sem=a2a_send_sem.at[g],
            recv_sem=a2a_recv_sem.at[g, int(g == LAST and k in FAR)],
            device_id=(me_o ^ k, me_l),
            device_id_type=MESH,
        )

    def a2a_bytes(g, count, far=0):
        return pltpu.make_async_remote_copy(
            src_ref=send_buf.at[g, pl.ds(0, count)],
            dst_ref=recv_buf.at[g, pl.ds(0, count)],
            send_sem=a2a_send_sem.at[g],
            recv_sem=a2a_recv_sem.at[g, far],
            device_id=(me_o ^ 1, me_l),
            device_id_type=MESH,
        )

    low = lax.broadcasted_iota(I32, (RANK, 128), 1) < RANK

    def both(a, b):
        return jnp.concatenate([a, b], axis=0)

    def diagonal(product):
        return jnp.where(low, product[:RANK], product[RANK:])

    def own_terms(k, c):
        for h in range(2):
            s0, s1 = c * CHUNK + h, c * CHUNK + 2 + h
            a = both(fac[s0, k, 0], fac[s1, k, 0])
            own[k, c, h] = diagonal(jnp.dot(a, state[k, c, h], preferred_element_type=F32))

    def start_event(c):
        for copy in all_loads[c][:2]:
            copy.wait()
        w = quad[...]
        for h in range(2):
            s0, s1 = c * CHUNK + h, c * CHUNK + 2 + h
            weighted = both(
                (four[s0].astype(F32) * w).astype(BF16), (four[s1].astype(F32) * w).astype(BF16)
            )
            basis = both(leaf[s0], leaf[s1])
            product = lax.dot_general(
                basis, weighted, (((1,), (1,)), ((), ())), preferred_element_type=F32
            )
            state[0, c, h] = diagonal(product).astype(BF16)

    def level_event(k, c):
        level_copy(k, c).wait_recv()
        for h in range(2):
            s0, s1 = c * CHUNK + h, c * CHUNK + 2 + h
            b = both(fac[s0, k, 1], fac[s1, k, 1])
            cross = diagonal(jnp.dot(b, partner[k, c, h], preferred_element_type=F32))
            present = jnp.where(low, spars[k, 0, s0], spars[k, 0, s1]).astype(F32)
            state[k + 1, c, h] = (own[k, c, h] + present * cross).astype(BF16)

    def a2a_event(g):
        x = [state[LEVELS, c].reshape(2 * RANK, 128) for c in GROUPS[g]]
        packed = lax.dot_general(
            perm[:, : 128 * len(x)],
            jnp.concatenate(x, axis=1),
            (((1,), (1,)), ((), ())),
            preferred_element_type=F32,
        ).astype(BF16)
        send_buf[g] = packed.reshape(N_ORDER, 16, 128)
        for k in sorted(NEAR + FAR, key=lambda k: -HOPS[k]):
            a2a_copy(g, k).start()
        recv_buf[g, 0] = send_buf[g, me_o]

    def prepare_perm():
        row = lax.broadcasted_iota(I32, (256, 256), 0)
        col = lax.broadcasted_iota(I32, (256, 256), 1)
        target = (row & 3) * 64 + (row >> 4) * 4 + ((row >> 2) & 3)
        perm[...] = (col == target).astype(F32).astype(BF16)

    def prepare_pick():
        small[2].wait()
        orders = order[...].astype(F32)
        for i in range(4):
            wide = jnp.broadcast_to(orders[i : i + 1], (128, 128))
            order_col[pl.ds(i * 128, 128)] = wide.T
        window = lax.broadcasted_iota(I32, (16, 512), 1).astype(F32)
        for g in range(SLOTS // 8):
            for q in range(4):
                for h in range(2):
                    col = order_col[pl.ds(8 * g + 2 * q + h, 16, stride=SLOTS), :]
                    wide = jnp.concatenate([col] * 4, axis=1)
                    row = g * 128 + q * 32 + h * 16
                    pick[pl.ds(row, 16)] = (wide == window).astype(F32).astype(BF16)
        pick_copy.start()

    def root_event(g):
        if g == 0:
            root_copy.wait()
        pair = len(GROUPS[g]) == 2
        row = lax.broadcasted_iota(I32, (32, 256), 0)
        col = lax.broadcasted_iota(I32, (32, 256), 1)
        keep = ((row >> 4) == ((col >> 6) & 1)) & ((row & 1) == (col >> 7))
        keep = keep.astype(F32).astype(BF16)
        first = (lax.broadcasted_iota(I32, (32, 128), 0) & 2) == 0

        def one(k):
            source = me_o ^ k
            r = recv_buf[g, k]
            r2 = jnp.concatenate([r, r], axis=1)
            lhs = jnp.concatenate([r2, r2], axis=0) * keep
            base = source * SLOTS + GROUPS[g][0] * CHUNK
            w = root[pl.ds(base, 4)].reshape(256, 128)
            if pair:
                w = jnp.concatenate([w, root[pl.ds(base + 4, 4)].reshape(256, 128)], axis=1)
            product = jnp.dot(lhs, w, preferred_element_type=F32)
            if pair:
                product = jnp.where(first, product[:, :128], product[:, 128:])
            coef[pl.ds(pl.multiple_of(source * 32, 32), 32)] = product

        if g == LAST:
            one(0)
            a2a_bytes(g, len(NEAR), 0).wait_recv()
            for k in NEAR:
                one(k)
            a2a_bytes(g, len(FAR), 1).wait_recv()
            for k in FAR:
                one(k)
        else:
            a2a_bytes(g, N_ORDER - 1).wait_recv()

            def body(k, carry):
                one(k)
                return carry

            lax.fori_loop(0, N_ORDER, body, 0, unroll=4)
        width = 128 if pair else 64
        lanes = pl.ds(GROUPS[g][0] * 64, width)
        for cc in range(4):
            parts = []
            for q in range(width // 32):
                for h in range(2):
                    parts.append(coef[pl.ds(h * 16 + cc * 4 + q, 16, stride=32), :])
            coef_t[cc, :, lanes] = jnp.concatenate(parts, axis=0).T.astype(BF16)
        if g == 2:
            part[...] = jnp.dot(
                coef_t[:, :, :384].reshape(512, 384), pick[:384], preferred_element_type=F32
            ).astype(BF16)
            part_copy.start()
        if g == LAST:
            coef_copy.start()

    coef_copy = pltpu.make_async_copy(coef_t.at[:, :, pl.ds(384, 128)], coef_hbm, out_sem.at[0])
    pick_copy = pltpu.make_async_copy(pick.at[pl.ds(384, 128)], pick_hbm, out_sem.at[1])
    part_copy = pltpu.make_async_copy(part, part_hbm, out_sem.at[2])

    small[0].wait()
    passed = False
    hold = (z == 1) | (z == 2)
    for event in schedule():
        if event[0] == "s" and event[1] == 0:
            c = event[2]
            start_event(c)
            if not passed:
                pl.semaphore_wait(barrier, len(neighbours))
                passed = True
            level_copy(0, c).start()
            if c == 0:
                tell(0)
        elif event[0] == "s":
            _, k, c = event
            if event == ("s", 1, 0):
                small[1].wait()
            if event in ROUNDS:
                hear(ROUNDS.index(event))
                if event != ROUNDS[-1]:
                    tell(ROUNDS.index(event) + 1)
            if k == 1:
                all_loads[c][2].wait()
                own_terms(0, c)
            level_event(k - 1, c)
            if k == LEVELS - 1:
                pl.when(jnp.logical_not(hold))(level_copy(k, c).start)
                own_terms(k, c)
            elif k < LEVELS:
                level_copy(k, c).start()
                own_terms(k, c)
        elif event[0] == "d":
            pl.when(hold)(level_copy(LEVELS - 1, event[1]).start)
        elif event[0] == "a":
            a2a_event(event[1])
        elif event[0] == "p":
            root_copy.start()
            prepare_perm()
            prepare_pick()
        else:
            root_event(event[1])
    for k in range(LEVELS):
        for c in range(CHUNKS):
            level_copy(k, c).wait_send()
    for g in range(len(GROUPS)):
        a2a_bytes(g, N_ORDER - 1).wait_send()
    for copy in (pick_copy, part_copy, coef_copy):
        copy.wait()


def finish_kernel(part_hbm, coef_hbm, pick_hbm, out_hbm, part, coef_t, pick, out, in_sem, out_sem):
    copies = [
        pltpu.make_async_copy(coef_hbm, coef_t, in_sem.at[0]),
        pltpu.make_async_copy(pick_hbm, pick, in_sem.at[1]),
    ] + [
        pltpu.make_async_copy(
            part_hbm.at[pl.ds(cc * 128, 128)], part.at[pl.ds(cc * 128, 128)], in_sem.at[2 + cc]
        )
        for cc in range(4)
    ]
    for copy in copies:
        copy.start()
    degree = lax.axis_index("lat") * 128 + lax.broadcasted_iota(I32, (128, 512), 0)
    window = DEGREES // 512 * lax.broadcasted_iota(I32, (128, 512), 1)
    alive = degree >= window
    for copy in copies[:2]:
        copy.wait()
    natural = jnp.dot(coef_t[...].reshape(512, 128), pick[...], preferred_element_type=F32)
    out_copies = []
    for cc in range(4):
        rows = slice(cc * 128, (cc + 1) * 128)
        copies[2 + cc].wait()
        total = part[rows].astype(F32) + natural[rows]
        out[cc] = jnp.where(alive, total, 0.0).astype(BF16)
        copy = pltpu.make_async_copy(out.at[cc], out_hbm.at[cc // 2, cc % 2], out_sem.at[cc])
        copy.start()
        out_copies.append(copy)
    for copy in out_copies:
        copy.wait()


def per_device(
    fourier, quad_weights, leaf_basis, level_factors, sparsity, root_basis, order_of_slot
):
    anywhere = pl.BlockSpec(memory_space=pl.ANY)
    vmem = pltpu.VMEM
    parts = pl.pallas_call(
        kernel,
        out_shape=[
            jax.ShapeDtypeStruct((512, 512), BF16),
            jax.ShapeDtypeStruct((4, 128, 128), BF16),
            jax.ShapeDtypeStruct((128, 512), BF16),
        ],
        in_specs=[anywhere] * 7,
        out_specs=[anywhere] * 3,
        scratch_shapes=[
            vmem((SLOTS, 64, 128), BF16),
            vmem((1, 128), F32),
            vmem((SLOTS, 64, 128), BF16),
            vmem((SLOTS, LEVELS, 2, 64, 64), BF16),
            pltpu.SMEM((LEVELS, 1, SLOTS), I32),
            vmem((512, 64, 128), BF16),
            vmem((4, 128), I32),
            vmem((LEVELS + 1, CHUNKS, 2, RANK, 128), BF16),
            vmem((LEVELS, CHUNKS, 2, RANK, 128), BF16),
            vmem((LEVELS, CHUNKS, 2, RANK, 128), F32),
            vmem((256, 256), BF16),
            vmem((len(GROUPS), N_ORDER, 16, 128), BF16),
            vmem((len(GROUPS), N_ORDER, 16, 128), BF16),
            vmem((512, 128), F32),
            vmem((512, 512), BF16),
            vmem((512, 128), F32),
            vmem((4, 128, 512), BF16),
            vmem((512, 512), BF16),
            pltpu.SemaphoreType.DMA((3, CHUNKS)),
            pltpu.SemaphoreType.DMA((3,)),
            pltpu.SemaphoreType.DMA,
            pltpu.SemaphoreType.DMA((3,)),
            pltpu.SemaphoreType.DMA((LEVELS, CHUNKS)),
            pltpu.SemaphoreType.DMA((LEVELS, CHUNKS)),
            pltpu.SemaphoreType.DMA((len(GROUPS),)),
            pltpu.SemaphoreType.DMA((len(GROUPS), 2)),
            pltpu.SemaphoreType.REGULAR((3,)),
        ],
        compiler_params=pltpu.CompilerParams(
            collective_id=0, has_side_effects=True, vmem_limit_bytes=60 * 1024 * 1024
        ),
        cost_estimate=pl.CostEstimate(
            flops=2 * 10**9, bytes_accessed=15 * 10**6, transcendentals=0
        ),
    )(
        fourier,
        quad_weights.reshape(1, 128),
        leaf_basis,
        level_factors,
        sparsity.transpose(1, 2, 0),
        root_basis,
        order_of_slot.reshape(4, 128),
    )
    return pl.pallas_call(
        finish_kernel,
        out_shape=jax.ShapeDtypeStruct((2, 2, 128, 512), BF16),
        in_specs=[anywhere] * 3,
        out_specs=anywhere,
        scratch_shapes=[
            vmem((512, 512), BF16),
            vmem((4, 128, 128), BF16),
            vmem((128, 512), BF16),
            vmem((4, 128, 512), BF16),
            pltpu.SemaphoreType.DMA((6,)),
            pltpu.SemaphoreType.DMA((4,)),
        ],
        compiler_params=pltpu.CompilerParams(vmem_limit_bytes=60 * 1024 * 1024),
        cost_estimate=pl.CostEstimate(
            flops=2**26, bytes_accessed=5 * 2**18, transcendentals=0
        ),
    )(*parts)


def solution(mesh):
    return jax.shard_map(
        per_device,
        mesh=mesh,
        in_specs=(
            P("order", None, "lat"),
            P("lat"),
            P("order", None, "lat"),
            P("order", None, None, "lat", None, None),
            P("order", None, "lat"),
            P(None, None, "lat"),
            P(),
        ),
        out_specs=P("order", None, "lat", None),
        check_vma=False,
    )
```
